256 devices in a mesh: grp: 8 (over z_hi, x), frame: 32 (over z_lo, y, core).
Axes of the slice: x: 4, y: 4, z: 8 (z_hi: 2, z_lo: 4; z = z_hi * 4 + z_lo), core: 2. Of those that a mesh axis runs over, the one named last changes fastest.
Arguments:
- hidden_states: bfloat16 [131072, 1280], P(('grp', 'frame')), may hold values from -6 to 6
- norm_gain: float32 [1280], replicated, may hold values from 0.1 to 1.9
- norm_bias: float32 [1280], replicated, may hold values from -3 to 3
- w_query: bfloat16 [1280, 640], replicated, may hold values from -3 to 3, as said below
- w_key: bfloat16 [1280, 640], replicated, may hold values from -3 to 3, as said below
- w_value: bfloat16 [1280, 640], replicated, may hold values from -0.15625 to 0.15625
- w_out: bfloat16 [640, 1280], replicated, may hold values from -0.25 to 0.25
- out_bias: float32 [1280], replicated, may hold values from -3 to 3
Outputs:
- block_out: bfloat16 [131072, 1280], P(('grp', 'frame'))
The draws below stay inside these ranges and needn't reach their ends.
Inputs may be any that keep to these rules, and one draw needn't show every extreme that they name: `w_query`: scaled by the fan-in. `w_key`: scaled by the fan-in.
All inputs are finite; a program needn't handle non-finite values.
Results may differ from the reference program's by a relative error of at most 0.0078.
Values may be sent and summed in bfloat16 or wider, within the bound.
No kernel may reach another device: no remote copies, remote signals or barrier semaphores. Data moves between devices by JAX's collectives and lax.ppermute only.
A program may use at most 128 MiB of HBM per device.

```python
import jax
import jax.numpy as jnp
from jax import lax

D = 1280
HEADS = 10
HEAD_DIM = 64
TOK = 512
INNER = 640
FRAMES = 256


def draw_w_query(key, part):
    key = jax.random.fold_in(key, 11)
    fresh = jax.random.truncated_normal(key, -4.0, 4.0, (D, HEADS * HEAD_DIM), jnp.float32) * D ** (-0.5)
    return fresh.astype(jnp.bfloat16)


def draw_w_key(key, part):
    key = jax.random.fold_in(key, 12)
    fresh = jax.random.truncated_normal(key, -4.0, 4.0, (D, HEADS * HEAD_DIM), jnp.float32) * D ** (-0.5)
    return fresh.astype(jnp.bfloat16)


def draw_hidden_states(key, part):
    key = jax.random.fold_in(key, 13)
    noise = jax.random.truncated_normal(jax.random.fold_in(key, 2), -5.0, 5.0, (FRAMES * TOK, D), jnp.float32)
    return noise.astype(jnp.bfloat16)


def scatter_about(rng, shape, scale, limit, dtype=jnp.bfloat16):
    return jnp.clip(scale * jax.random.normal(rng, shape, jnp.float32), -limit, limit).astype(dtype)


def setup_inputs(seed: int = 0) -> dict:
    arg_keys = jax.random.split(jax.random.key(seed), 9)
    hidden_states = draw_hidden_states(jax.random.fold_in(arg_keys[8], 71), 0)
    norm_gain = jnp.clip(1.0 + 0.18 * jax.random.normal(arg_keys[1], (D,), jnp.float32), 0.1, 1.9)
    norm_bias = scatter_about(arg_keys[2], (D,), 0.5, 3.0, jnp.float32)
    w_query = draw_w_query(jax.random.fold_in(arg_keys[8], 71), 0)
    w_key = draw_w_key(jax.random.fold_in(arg_keys[8], 71), 0)
    w_value = scatter_about(arg_keys[5], (D, INNER), D ** -0.5, 0.15625)
    w_out = scatter_about(arg_keys[6], (INNER, D), INNER ** -0.5, 0.25)
    out_bias = scatter_about(arg_keys[7], (D,), 0.5, 3.0, jnp.float32)
    return {"hidden_states": hidden_states, "norm_gain": norm_gain, "norm_bias": norm_bias, "w_query": w_query, "w_key": w_key, "w_value": w_value, "w_out": w_out, "out_bias": out_bias}


def layer_norm(rows, norm_gain, norm_bias):
    values32 = rows.astype(jnp.float32)
    center = lax.optimization_barrier(jnp.mean(values32, axis=-1, keepdims=True))
    spread = lax.optimization_barrier(jnp.mean((values32 - center) ** 2, axis=-1, keepdims=True))
    return ((values32 - center) * lax.rsqrt(spread + 1e-05) * norm_gain + norm_bias).astype(jnp.bfloat16)

def attend(query, context_keys, context_values):
    tokens = query.shape[0]
    q_heads = query.reshape(tokens, HEADS, HEAD_DIM).astype(jnp.float32)
    k_heads = context_keys.reshape(-1, HEADS, HEAD_DIM).astype(jnp.float32)
    v_heads = context_values.reshape(-1, HEADS, HEAD_DIM).astype(jnp.float32)
    scores = jnp.einsum('qhd,khd->hqk', q_heads, k_heads) * HEAD_DIM ** (-0.5)
    top = lax.optimization_barrier(jnp.max(scores, axis=-1, keepdims=True))
    raised = jnp.exp(scores - top)
    weights = (raised / lax.optimization_barrier(jnp.sum(raised, axis=-1, keepdims=True))).astype(jnp.bfloat16)
    mixed = jnp.einsum('hqk,khd->qhd', weights.astype(jnp.float32), v_heads)
    return mixed.reshape(tokens, HEADS * HEAD_DIM).astype(jnp.bfloat16)

def reference(hidden_states, norm_gain, norm_bias, w_query, w_key, w_value, w_out, out_bias):
    normed = layer_norm(hidden_states, norm_gain, norm_bias)
    query = jnp.dot(normed, w_query, preferred_element_type=jnp.float32).astype(jnp.bfloat16)
    keys = jnp.dot(normed, w_key, preferred_element_type=jnp.float32).astype(jnp.bfloat16)
    values = jnp.dot(normed, w_value, preferred_element_type=jnp.float32).astype(jnp.bfloat16)
    query = query.reshape(FRAMES, TOK, HEADS * HEAD_DIM)
    keys = keys.reshape(FRAMES, TOK, HEADS * HEAD_DIM)
    values = values.reshape(FRAMES, TOK, HEADS * HEAD_DIM)
    prior_keys = jnp.concatenate([keys[:1], keys[:-1]], axis=0)
    prior_values = jnp.concatenate([values[:1], values[:-1]], axis=0)

    def one_frame(packed):
        frame_query, frame_keys, frame_values = packed
        context_keys = jnp.concatenate([keys[0], frame_keys], axis=0)
        context_values = jnp.concatenate([values[0], frame_values], axis=0)
        return attend(frame_query, context_keys, context_values)
    attended = lax.map(one_frame, (query, prior_keys, prior_values))
    attended = attended.reshape(FRAMES * TOK, HEADS * HEAD_DIM)
    projected = jnp.dot(attended, w_out, preferred_element_type=jnp.float32)
    total = hidden_states.astype(jnp.float32) + projected + out_bias
    return total.astype(jnp.bfloat16)
```

```python
import jax
import jax.numpy as jnp
import numpy as np
from jax import lax
from jax.sharding import PartitionSpec as P

HEADS = 10
HEAD_DIM = 64
AXES = ("grp", "frame")


SIZES = {"x": 4, "y": 4, "z": 8}
RING_STEPS = {
    4: (
        (((0, 0), (1, 0)), ((2, 0), (3, 0)), ((0, 1), (3, 1)), ((1, 1), (2, 1))),
        (((0, 0), (3, 0)), ((1, 0), (2, 0)), ((0, 1), (1, 1)), ((2, 1), (3, 1))),
    ),
    8: (
        (((0, 0), (3, 0)), ((0, 1), (5, 1)), ((3, 1), (5, 0))),
        (
            ((0, 0), (6, 0)), ((3, 0), (4, 0)), ((0, 1), (2, 1)), ((5, 1), (4, 1)),
            ((2, 0), (3, 1)), ((5, 0), (6, 1)),
        ),
        (
            ((0, 0), (1, 0)), ((2, 0), (3, 0)), ((4, 0), (5, 0)), ((6, 0), (7, 0)),
            ((0, 1), (7, 1)), ((5, 1), (6, 1)), ((3, 1), (4, 1)), ((1, 1), (2, 1)),
        ),
    ),
}


def device_index(x, y, z, core):
    return ((z // 4) * 4 + x) * 32 + ((z % 4) * 4 + y) * 2 + core


def tree(order):
    holders = {(0, 0, 0, 0), (0, 0, 0, 1)}
    joined = np.full(256, -1, np.int32)
    taken = {"x": 0, "y": 0, "z": 0}
    rounds = []
    for step, axis in enumerate(order):
        pairs = RING_STEPS[SIZES[axis]][taken[axis]]
        taken[axis] += 1
        place = "xyz".index(axis)
        target = [i ^ 1 for i in range(256)]
        lines = {h[:place] + h[place + 1 : 3] for h in holders}
        fresh = set()
        for line in lines:
            for (a, core_a), (b, core_b) in pairs:
                first = line[:place] + (a,) + line[place:] + (core_a,)
                second = line[:place] + (b,) + line[place:] + (core_b,)
                target[device_index(*first)] = device_index(*second)
                target[device_index(*second)] = device_index(*first)
                for source, sink in ((first, second), (second, first)):
                    if core_a == core_b and source in holders and sink not in holders:
                        fresh.add(sink)
                        joined[device_index(*sink)] = step
        holders |= fresh
        rounds.append([(i, target[i]) for i in range(256)])
        assert sorted(target) == list(range(256))
        assert all(i != t for i, t in rounds[-1])
    assert len(holders) == 256
    return rounds, joined


CORE_SWAP = [(i, i ^ 1) for i in range(256)]
NEXT_FRAME = [(i, (i + 1) % 256) for i in range(256)]

ORDERS = ("zzzxxyy", "xxyyzzz", "yyzzzxx")
CHUNKS = (96, 80, 80)


def from_first(rows, position):
    plans = [tree(order) for order in ORDERS]
    table = np.stack([joined for _, joined in plans])
    mine = lax.dynamic_slice_in_dim(jnp.asarray(table), position, 1, axis=1)[:, 0]
    half = rows.shape[0] // 2
    other = lax.ppermute(rows[half:], AXES, CORE_SWAP)
    start = jnp.where(position % 2 == 1, other, rows[:half])
    held = jnp.split(start, np.cumsum(CHUNKS)[:-1], axis=0)
    for step in range(len(ORDERS[0])):
        for which, (rounds, _) in enumerate(plans):
            come = lax.ppermute(held[which], AXES, rounds[step])
            held[which] = jnp.where(mine[which] == step, come, held[which])
    return held + [lax.ppermute(piece, AXES, CORE_SWAP) for piece in held]


def layer_norm(rows, norm_gain, norm_bias):
    values32 = rows.astype(jnp.float32)
    center = jnp.mean(values32, axis=-1, keepdims=True)
    spread = jnp.mean((values32 - center) ** 2, axis=-1, keepdims=True)
    return ((values32 - center) * lax.rsqrt(spread + 1e-05) * norm_gain + norm_bias).astype(
        jnp.bfloat16
    )


def project(rows, weight):
    return jnp.dot(rows, weight, preferred_element_type=jnp.float32).astype(jnp.bfloat16)


def attend(query, context_keys, context_values):
    tokens = query.shape[0]
    q_heads = query.reshape(tokens, HEADS, HEAD_DIM)
    k_heads = context_keys.reshape(-1, HEADS, HEAD_DIM)
    v_heads = context_values.reshape(-1, HEADS, HEAD_DIM)
    scores = jnp.einsum(
        "qhd,khd->hqk", q_heads, k_heads, preferred_element_type=jnp.float32
    ) * HEAD_DIM ** (-0.5)
    top = jnp.max(scores, axis=-1, keepdims=True)
    raised = jnp.exp(scores - top)
    weights = (raised / jnp.sum(raised, axis=-1, keepdims=True)).astype(jnp.bfloat16)
    mixed = jnp.einsum("hqk,khd->qhd", weights, v_heads, preferred_element_type=jnp.float32)
    return mixed.reshape(tokens, HEADS * HEAD_DIM).astype(jnp.bfloat16)


def body(hidden_states, norm_gain, norm_bias, w_query, w_key, w_value, w_out, out_bias):
    position = lax.axis_index("grp") * lax.axis_size("frame") + lax.axis_index("frame")
    shifted = lax.ppermute(hidden_states, AXES, NEXT_FRAME)
    leading = from_first(hidden_states, position)
    query = project(layer_norm(hidden_states, norm_gain, norm_bias), w_query)
    prior = jnp.where(position == 0, hidden_states, shifted)
    context = jnp.concatenate(leading + [prior], axis=0)
    normed = layer_norm(context, norm_gain, norm_bias)
    attended = attend(query, project(normed, w_key), project(normed, w_value))
    projected = jnp.dot(attended, w_out, preferred_element_type=jnp.float32)
    total = hidden_states.astype(jnp.float32) + projected + out_bias
    return total.astype(jnp.bfloat16)


def solution(mesh):
    placed = (P(AXES, None), P(), P(), P(), P(), P(), P(), P())
    return jax.shard_map(
        body, mesh=mesh, in_specs=placed, out_specs=P(AXES, None), check_vma=False
    )
```

```python
import jax
import jax.numpy as jnp
from jax import lax
from jax.sharding import PartitionSpec as P

HEADS = 10
HEAD_DIM = 64
AXES = ("grp", "frame")


SIZES = {"x": 4, "y": 4, "z": 8}

EVEN4 = (((0, 0), (1, 0)), ((2, 0), (3, 0)), ((0, 1), (3, 1)), ((1, 1), (2, 1)))
ODD4 = (((0, 0), (3, 0)), ((1, 0), (2, 0)), ((0, 1), (1, 1)), ((2, 1), (3, 1)))
EVEN8 = (
    ((0, 0), (1, 0)), ((2, 0), (3, 0)), ((4, 0), (5, 0)), ((6, 0), (7, 0)),
    ((0, 1), (7, 1)), ((5, 1), (6, 1)), ((3, 1), (4, 1)), ((1, 1), (2, 1)),
)
ODD8 = (
    ((0, 0), (7, 0)), ((5, 0), (6, 0)), ((3, 0), (4, 0)), ((1, 0), (2, 0)),
    ((0, 1), (1, 1)), ((2, 1), (3, 1)), ((4, 1), (5, 1)), ((6, 1), (7, 1)),
)
HALF8 = (((0, 0), (4, 0)), ((0, 1), (4, 1)))
FIRST8 = (((0, 0), (3, 0)), ((0, 1), (5, 1)), ((3, 1), (5, 0)))
SECOND8 = (
    ((0, 0), (6, 0)), ((3, 0), (4, 0)), ((0, 1), (2, 1)), ((5, 1), (4, 1)),
    ((2, 0), (3, 1)), ((5, 0), (6, 1)),
)


def device_index(x, y, z, core):
    return ((z // 4) * 4 + x) * 32 + ((z % 4) * 4 + y) * 2 + core


def permutation(axis, pairs, lines):
    place = "xyz".index(axis)
    target = [i ^ 1 for i in range(256)]
    for line in lines:
        for (a, core_a), (b, core_b) in pairs:
            first = device_index(*line[:place], a, *line[place:], core_a)
            second = device_index(*line[:place], b, *line[place:], core_b)
            target[first], target[second] = second, first
    assert sorted(target) == list(range(256))
    assert all(target[i] != i for i in range(256))
    return [(i, target[i]) for i in range(256)]


def all_lines(axis):
    sizes = [SIZES[other] for other in "xyz" if other != axis]
    return [(a, b) for a in range(sizes[0]) for b in range(sizes[1])]


def tree(steps):
    held = {"x": {0}, "y": {0}, "z": {0}}
    rounds = []
    for axis, pairs in steps:
        others = [other for other in "xyz" if other != axis]
        lines = set()
        for a in held[others[0]]:
            for b in held[others[1]]:
                lines.add((a, b))
                lines.add((-a % SIZES[others[0]], -b % SIZES[others[1]]))
        if len({end for pair in pairs for end in pair}) == 2 * SIZES[axis]:
            lines = all_lines(axis)
        before = {name: sum(1 << v for v in nodes) for name, nodes in held.items()}
        rounds.append((permutation(axis, pairs, lines), before))
        fresh = set()
        for (a, core_a), (b, core_b) in pairs:
            if core_a == core_b == 0:
                fresh |= {b} if a in held[axis] else set()
                fresh |= {a} if b in held[axis] else set()
        held[axis] = held[axis] | fresh
    assert all(len(held[name]) == SIZES[name] for name in "xyz")
    return rounds


CORE_SWAP = [(i, i ^ 1) for i in range(256)]
NEXT_FRAME = [(i, (i + 1) % 256) for i in range(256)]
X, Y = [("x", EVEN4), ("x", ODD4)], [("y", EVEN4), ("y", ODD4)]
Z = [("z", FIRST8), ("z", SECOND8), ("z", EVEN8)]
PLANS = (
    (96, X + Y + Z, 0),
    (96, Y + Z + X, 0),
    (64, [("z", HALF8), ("z", EVEN8), ("z", ODD8)] + X + Y, 1),
)


def from_first(rows):
    grp, frame = lax.axis_index("grp"), lax.axis_index("frame")
    core = frame % 2
    place = {"x": grp % 4, "y": frame // 2 % 4, "z": grp // 4 * 4 + frame // 8}
    place = {n: jnp.where(core == 1, (SIZES[n] - v) % SIZES[n], v) for n, v in place.items()}

    def holds(before):
        inside = [(before[n] >> place[n]) & 1 for n in "xyz"]
        return inside[0] * inside[1] * inside[2] == 1

    half = rows.shape[0] // 2
    other = lax.ppermute(rows, AXES, CORE_SWAP)
    pieces, start = [], 0
    for size, _, _ in PLANS:
        pieces.append(
            jnp.where(
                core == 1, other[half + start : half + start + size], rows[start : start + size]
            )
        )
        start += size
    trees = [tree(steps) for _, steps, _ in PLANS]
    for step in range(len(trees[0])):
        for which, (_, _, skip) in enumerate(PLANS):
            if step == len(trees[which]):
                continue
            pairs, before = trees[which][step]
            piece = pieces[which]
            if skip <= step < skip + 2:
                middle = piece.shape[0] // 2
                piece, sent = piece[:middle], piece[middle:]
            else:
                sent = piece
            come = lax.ppermute(sent, AXES, pairs)
            pieces[which] = jnp.where(holds(before), piece, come)
    for back in (1, 0):
        for which, (_, steps, skip) in enumerate(PLANS):
            axis, pairs = steps[skip + back]
            come = lax.ppermute(
                pieces[which], AXES, permutation(axis, pairs, all_lines(axis))
            )
            pieces[which] = jnp.concatenate([pieces[which], come], axis=0)
    return pieces + [lax.ppermute(piece, AXES, CORE_SWAP) for piece in pieces]


def layer_norm(rows, norm_gain, norm_bias):
    values32 = rows.astype(jnp.float32)
    center = jnp.mean(values32, axis=-1, keepdims=True)
    spread = jnp.mean((values32 - center) ** 2, axis=-1, keepdims=True)
    return ((values32 - center) * lax.rsqrt(spread + 1e-05) * norm_gain + norm_bias).astype(
        jnp.bfloat16
    )


def project(rows, weight):
    return jnp.dot(rows, weight, preferred_element_type=jnp.float32).astype(jnp.bfloat16)


def attend(query, context_keys, context_values):
    tokens = query.shape[0]
    q_heads = query.reshape(tokens, HEADS, HEAD_DIM)
    k_heads = context_keys.reshape(-1, HEADS, HEAD_DIM)
    v_heads = context_values.reshape(-1, HEADS, HEAD_DIM)
    scores = jnp.einsum(
        "qhd,khd->hqk", q_heads, k_heads, preferred_element_type=jnp.float32
    ) * HEAD_DIM ** (-0.5)
    top = jnp.max(scores, axis=-1, keepdims=True)
    raised = jnp.exp(scores - top)
    weights = (raised / jnp.sum(raised, axis=-1, keepdims=True)).astype(jnp.bfloat16)
    mixed = jnp.einsum("hqk,khd->qhd", weights, v_heads, preferred_element_type=jnp.float32)
    return mixed.reshape(tokens, HEADS * HEAD_DIM).astype(jnp.bfloat16)


def body(hidden_states, norm_gain, norm_bias, w_query, w_key, w_value, w_out, out_bias):
    position = lax.axis_index("grp") * lax.axis_size("frame") + lax.axis_index("frame")
    shifted = lax.ppermute(hidden_states, AXES, NEXT_FRAME)
    leading = from_first(hidden_states)
    query = project(layer_norm(hidden_states, norm_gain, norm_bias), w_query)
    prior = jnp.where(position == 0, hidden_states, shifted)
    context = jnp.concatenate(leading + [prior], axis=0)
    normed = layer_norm(context, norm_gain, norm_bias)
    attended = attend(query, project(normed, w_key), project(normed, w_value))
    projected = jnp.dot(attended, w_out, preferred_element_type=jnp.float32)
    total = hidden_states.astype(jnp.float32) + projected + out_bias
    return total.astype(jnp.bfloat16)


def solution(mesh):
    placed = (P(AXES, None), P(), P(), P(), P(), P(), P(), P())
    return jax.shard_map(
        body, mesh=mesh, in_specs=placed, out_specs=P(AXES, None), check_vma=False
    )
```

```python
import jax
import jax.numpy as jnp
from jax import lax
from jax.experimental import pallas as pl
from jax.experimental.pallas import tpu as pltpu
from jax.sharding import PartitionSpec as P

HEADS = 10
HEAD_DIM = 64
PAIR = 2 * HEAD_DIM
BLOCK = 256
VMEM_BYTES = 40 << 20
AXES = ("grp", "frame")
EARLY = 5


SIZES = {"x": 4, "y": 4, "z": 8}

STEPS = {
    4: (((0, 1),), ((0, 3), (1, 2))),
    8: (((0, 3),), ((0, 6), (3, 4)), ((0, 1), (3, 2), (4, 5), (6, 7))),
}
ORDER = "xxzzzyy"
SPLITS = 2


def device_index(place, core):
    if core == 1:
        place = {n: -v % SIZES[n] for n, v in place.items()}
    x, y, z = place["x"], place["y"], place["z"]
    return ((z // 4) * 4 + x) * 32 + ((z % 4) * 4 + y) * 2 + core


def tree():
    held = {name: [0] for name in "xyz"}
    taken = {name: 0 for name in "xyz"}
    rounds = []
    for axis in ORDER:
        step = STEPS[SIZES[axis]][taken[axis]]
        taken[axis] += 1
        pairs = []
        for core in range(2):
            for x in held["x"]:
                for y in held["y"]:
                    for z in held["z"]:
                        place = {"x": x, "y": y, "z": z}
                        for source, sink in step:
                            if place[axis] == source:
                                pairs.append(
                                    (
                                        device_index(place, core),
                                        device_index({**place, axis: sink}, core),
                                    )
                                )
        before = {name: sum(1 << v for v in nodes) for name, nodes in held.items()}
        rounds.append((sorted(pairs), before))
        held[axis] = held[axis] + [sink for _, sink in step]
    assert all(len(held[name]) == SIZES[name] for name in "xyz")
    return rounds


def exchange(step):
    pairs = []
    for core in range(2):
        for y in range(4):
            for z in range(8):
                for a, b in (((0, 1), (2, 3)), ((0, 3), (1, 2)))[step]:
                    ends = [device_index({"x": v, "y": y, "z": z}, core) for v in (a, b)]
                    pairs += [(ends[0], ends[1]), (ends[1], ends[0])]
    return sorted(pairs)


CORE_SWAP = [(i, i ^ 1) for i in range(256)]
NEXT_FRAME = [(i, (i + 1) % 256) for i in range(256)]


def holding():
    grp, frame = lax.axis_index("grp"), lax.axis_index("frame")
    core = frame % 2
    place = {"x": grp % 4, "y": frame // 2 % 4, "z": grp // 4 * 4 + frame // 8}
    place = {n: jnp.where(core == 1, (SIZES[n] - v) % SIZES[n], v) for n, v in place.items()}

    def holds(before):
        inside = [(before[n] >> place[n]) & 1 for n in "xyz"]
        return inside[0] * inside[1] * inside[2] == 1

    return core == 1, holds


def scatter(rows):
    second, holds = holding()
    quarter = rows.shape[0] // 4
    quarters = [rows[quarter * i : quarter * (i + 1)] for i in range(4)]
    sinks = [device_index({"x": 1, "y": 0, "z": 0}, core) for core in range(2)]
    near = lax.ppermute(quarters[1], AXES, [(0, sinks[0])])
    far = lax.ppermute(quarters[3], AXES, [(0, sinks[1])])
    other = lax.ppermute(quarters[2], AXES, CORE_SWAP)
    return jnp.where(
        holds({n: 1 for n in "xyz"}),
        jnp.where(second, other, quarters[0]),
        jnp.where(second, far, near),
    )


def spread(piece, steps):
    _, holds = holding()
    rounds = tree()
    for step in steps:
        pairs, before = rounds[step]
        sent = piece
        if step < SPLITS:
            middle = piece.shape[0] // 2
            piece, sent = piece[:middle], piece[middle:]
        come = lax.ppermute(sent, AXES, pairs)
        piece = jnp.where(holds(before), piece, come)
    return piece


def gather(piece):
    for step in reversed(range(SPLITS)):
        come = lax.ppermute(piece, AXES, exchange(step))
        piece = jnp.concatenate([piece, come], axis=0)
    return piece


def normed(rows, gain, bias):
    values = rows.astype(jnp.float32)
    center = jnp.mean(values, axis=-1, keepdims=True)
    values = values - center
    spread = jnp.mean(values * values, axis=-1, keepdims=True)
    return (values * lax.rsqrt(spread + 1e-05) * gain + bias).astype(jnp.bfloat16)


def project(rows, weight):
    return jnp.dot(rows, weight, preferred_element_type=jnp.float32)


def query_kernel(rows_ref, gain_ref, bias_ref, weight_ref, out_ref):
    rows = normed(rows_ref[...], gain_ref[...], bias_ref[...])
    query = project(rows, weight_ref[...]).astype(jnp.bfloat16)
    out_ref[...] = query * jnp.bfloat16(HEAD_DIM ** (-0.5))


def pair_lanes(shape):
    return lax.broadcasted_iota(jnp.int32, shape, 1) < HEAD_DIM


def context(rows, gain, bias, key_ref, value_ref):
    rows = normed(rows, gain, bias)
    keys = project(rows, key_ref[...]).astype(jnp.bfloat16)
    values = project(rows, value_ref[...]).astype(jnp.bfloat16)
    lane = lax.broadcasted_iota(jnp.int32, (rows.shape[0], PAIR), 1)
    first = lane < HEAD_DIM
    none = jnp.zeros((rows.shape[0], PAIR), jnp.bfloat16)
    heads = []
    for pair in range(HEADS // 2):
        columns = slice(pair * PAIR, (pair + 1) * PAIR)
        key, value = keys[:, columns], values[:, columns]
        one_right = jnp.where(lane == HEAD_DIM, 1.0, 0.0).astype(jnp.bfloat16)
        one_left = jnp.where(lane == 0, 1.0, 0.0).astype(jnp.bfloat16)
        heads.append((jnp.where(first, key, none), jnp.where(first, value, one_right)))
        heads.append((jnp.where(first, none, key), jnp.where(first, one_left, value)))
    return heads


def attend(query, key, value):
    scores = lax.dot_general(
        query, key, (((1,), (1,)), ((), ())), preferred_element_type=jnp.float32
    )
    top = jnp.max(scores, axis=-1, keepdims=True)
    raised = jnp.exp(scores - top).astype(jnp.bfloat16)
    return jnp.dot(raised, value, preferred_element_type=jnp.float32), top


def part_kernel(
    first_ref, rows_ref, own_ref, query_ref, gain_ref, bias_ref, key_ref, value_ref, sum_ref, top_ref
):
    rows = jnp.where(first_ref[0] == 1, own_ref[...], rows_ref[...])
    heads = context(rows, gain_ref[...], bias_ref[...], key_ref, value_ref)
    for start in range(0, query_ref.shape[0], BLOCK):
        block = pl.ds(start, BLOCK)
        tops = []
        for head, (key, value) in enumerate(heads):
            pair = head // 2
            mixed, top = attend(query_ref[block, pair * PAIR : (pair + 1) * PAIR], key, value)
            sum_ref[block, head * PAIR : (head + 1) * PAIR] = mixed
            tops.append(top)
        top_ref[block, :] = jnp.concatenate(
            tops + [jnp.zeros((BLOCK, PAIR - HEADS), jnp.float32)], axis=1
        )


def last_kernel(
    rows_ref, query_ref, gain_ref, bias_ref, key_ref, value_ref,
    sum_a_ref, top_a_ref, sum_b_ref, top_b_ref, hidden_ref, out_weight_ref, out_bias_ref, out_ref,
):
    heads = context(rows_ref[...], gain_ref[...], bias_ref[...], key_ref, value_ref)
    for start in range(0, query_ref.shape[0], BLOCK):
        block = pl.ds(start, BLOCK)
        left = pair_lanes((BLOCK, PAIR))
        mixed = []
        for pair in range(HEADS // 2):
            query = query_ref[block, pair * PAIR : (pair + 1) * PAIR]
            parts = []
            for head in (2 * pair, 2 * pair + 1):
                columns = slice(head * PAIR, (head + 1) * PAIR)
                total, top = attend(query, *heads[head])
                top_a, top_b = top_a_ref[block, head : head + 1], top_b_ref[block, head : head + 1]
                most = jnp.maximum(top, jnp.maximum(top_a, top_b))
                total = (
                    total * jnp.exp(top - most)
                    + sum_a_ref[block, columns] * jnp.exp(top_a - most)
                    + sum_b_ref[block, columns] * jnp.exp(top_b - most)
                )
                ones = HEAD_DIM if head % 2 == 0 else 0
                parts.append(total / total[:, ones : ones + 1])
            mixed.append(jnp.where(left, parts[0], parts[1]).astype(jnp.bfloat16))
        attended = jnp.concatenate(mixed, axis=1)
        projected = project(attended, out_weight_ref[...])
        total = hidden_ref[block, :].astype(jnp.float32) + projected + out_bias_ref[...]
        out_ref[block, :] = total.astype(jnp.bfloat16)


def call(kernel, outs, *operands, scalars=0, flops=0, exps=0):
    whole = pl.BlockSpec(memory_space=pltpu.VMEM)
    specs = [pl.BlockSpec(memory_space=pltpu.SMEM)] * scalars
    return pl.pallas_call(
        kernel,
        out_shape=outs,
        in_specs=specs + [whole] * (len(operands) - scalars),
        out_specs=jax.tree.map(lambda _: whole, outs),
        compiler_params=pltpu.CompilerParams(vmem_limit_bytes=VMEM_BYTES),
        cost_estimate=pl.CostEstimate(flops=flops, bytes_accessed=8 << 20, transcendentals=exps),
    )(*operands)


def body(hidden_states, norm_gain, norm_bias, w_query, w_key, w_value, w_out, out_bias):
    position = lax.axis_index("grp") * lax.axis_size("frame") + lax.axis_index("frame")
    at_start = jnp.where(position == 0, 1, 0).astype(jnp.int32).reshape(1)
    gain, bias = norm_gain.reshape(1, -1), norm_bias.reshape(1, -1)
    tokens, width = hidden_states.shape
    inner = w_query.shape[1]
    shifted = lax.ppermute(hidden_states, AXES, NEXT_FRAME)
    piece = scatter(hidden_states)
    query = call(
        query_kernel, jax.ShapeDtypeStruct((tokens, inner), jnp.bfloat16),
        hidden_states, gain, bias, w_query, flops=2 * tokens * width * inner,
    )
    piece = spread(piece, range(1, EARLY))
    piece, shifted, query = lax.optimization_barrier((piece, shifted, query))
    partial = (
        jax.ShapeDtypeStruct((tokens, HEADS * PAIR), jnp.float32),
        jax.ShapeDtypeStruct((tokens, PAIR), jnp.float32),
    )

    def part(rows, own, flag):
        return call(
            part_kernel, partial, flag, rows, own, query, gain, bias, w_key, w_value,
            scalars=1, flops=4 * rows.shape[0] * inner * (width + 8 * tokens),
            exps=rows.shape[0] * tokens * HEADS,
        )

    prior = part(shifted, hidden_states, at_start)
    piece = spread(piece, range(EARLY, len(ORDER)))
    half = gather(piece)
    other = lax.ppermute(half, AXES, CORE_SWAP)
    near = part(half, half, jnp.zeros((1,), jnp.int32))
    return call(
        last_kernel, jax.ShapeDtypeStruct((tokens, width), jnp.bfloat16),
        other, query, gain, bias, w_key, w_value, *prior, *near,
        hidden_states, w_out, out_bias.reshape(1, -1),
        flops=4 * other.shape[0] * inner * (width + 8 * tokens),
    )


def solution(mesh):
    placed = (P(AXES, None), P(), P(), P(), P(), P(), P(), P())
    return jax.shard_map(
        body, mesh=mesh, in_specs=placed, out_specs=P(AXES, None), check_vma=False
    )
```

```python
import functools

import jax
import jax.numpy as jnp
from jax import lax
from jax.experimental import pallas as pl
from jax.experimental.pallas import tpu as pltpu
from jax.sharding import PartitionSpec as P

HEADS = 10
HEAD_DIM = 64
PAIR = 2 * HEAD_DIM
HALF = HEADS // 2
OUT_TILE = 256
VMEM_BYTES = 40 << 20
AXES = ("grp", "frame")


SIZES = {"x": 4, "y": 4, "z": 8}

STEPS = {
    4: (((0, 1),), ((0, 3), (1, 2))),
    8: (((0, 3),), ((0, 6), (3, 4)), ((0, 1), (3, 2), (4, 5), (6, 7))),
}
ORDER = "xxzzzyy"
SPLITS = 2


def device_index(place, core):
    if core == 1:
        place = {n: -v % SIZES[n] for n, v in place.items()}
    x, y, z = place["x"], place["y"], place["z"]
    return ((z // 4) * 4 + x) * 32 + ((z % 4) * 4 + y) * 2 + core


def tree():
    held = {name: [0] for name in "xyz"}
    taken = {name: 0 for name in "xyz"}
    rounds = []
    for axis in ORDER:
        step = STEPS[SIZES[axis]][taken[axis]]
        taken[axis] += 1
        pairs = []
        for core in range(2):
            for x in held["x"]:
                for y in held["y"]:
                    for z in held["z"]:
                        place = {"x": x, "y": y, "z": z}
                        for source, sink in step:
                            if place[axis] == source:
                                pairs.append(
                                    (
                                        device_index(place, core),
                                        device_index({**place, axis: sink}, core),
                                    )
                                )
        before = {name: sum(1 << v for v in nodes) for name, nodes in held.items()}
        rounds.append((sorted(pairs), before))
        held[axis] = held[axis] + [sink for _, sink in step]
    assert all(len(held[name]) == SIZES[name] for name in "xyz")
    return rounds


def exchange(step):
    pairs = []
    for core in range(2):
        for y in range(4):
            for z in range(8):
                for a, b in (((0, 1), (2, 3)), ((0, 3), (1, 2)))[step]:
                    ends = [device_index({"x": v, "y": y, "z": z}, core) for v in (a, b)]
                    pairs += [(ends[0], ends[1]), (ends[1], ends[0])]
    return sorted(pairs)


CORE_SWAP = [(i, i ^ 1) for i in range(256)]
NEXT_FRAME = [(i, (i + 1) % 256) for i in range(256)]


def holding():
    grp, frame = lax.axis_index("grp"), lax.axis_index("frame")
    core = frame % 2
    place = {"x": grp % 4, "y": frame // 2 % 4, "z": grp // 4 * 4 + frame // 8}
    place = {n: jnp.where(core == 1, (SIZES[n] - v) % SIZES[n], v) for n, v in place.items()}

    def holds(before):
        inside = [(before[n] >> place[n]) & 1 for n in "xyz"]
        return inside[0] * inside[1] * inside[2] == 1

    return core == 1, holds


def scatter(rows):
    second, holds = holding()
    quarter = rows.shape[0] // 4
    quarters = [rows[quarter * i : quarter * (i + 1)] for i in range(4)]
    sinks = [device_index({"x": 1, "y": 0, "z": 0}, core) for core in range(2)]
    near = lax.ppermute(quarters[1], AXES, [(0, sinks[0])])
    far = lax.ppermute(quarters[3], AXES, [(0, sinks[1])])
    other = lax.ppermute(quarters[2], AXES, CORE_SWAP)
    return jnp.where(
        holds({n: 1 for n in "xyz"}),
        jnp.where(second, other, quarters[0]),
        jnp.where(second, far, near),
    )


def spread(piece, steps):
    _, holds = holding()
    rounds = tree()
    for step in steps:
        pairs, before = rounds[step]
        sent = piece
        if step < SPLITS:
            middle = piece.shape[0] // 2
            piece, sent = piece[:middle], piece[middle:]
        come = lax.ppermute(sent, AXES, pairs)
        piece = jnp.where(holds(before), piece, come)
    return piece


def normed(rows, gain, bias):
    values = rows.astype(jnp.float32)
    center = jnp.mean(values, axis=-1, keepdims=True)
    values = values - center
    spread = jnp.mean(values * values, axis=-1, keepdims=True)
    return (values * lax.rsqrt(spread + 1e-05) * gain + bias).astype(jnp.bfloat16)


def project(rows, weight):
    return jnp.dot(rows, weight, preferred_element_type=jnp.float32)


def lanes_of(rows):
    return lax.broadcasted_iota(jnp.int32, (rows, PAIR), 1)


def columns(index):
    return slice(index * PAIR, (index + 1) * PAIR)


def own_lanes(head, array, fill):
    left = lanes_of(array.shape[0]) < HEAD_DIM
    other = jnp.full(array.shape, fill, jnp.bfloat16)
    return jnp.where(left, array, other) if head % 2 == 0 else jnp.where(left, other, array)


def attend(head, query, key, value, carried=None):
    scores = lax.dot_general(
        query, own_lanes(head, key, 0.0), (((1,), (1,)), ((), ())),
        preferred_element_type=jnp.float32,
    )
    tiles = [scores[:, i : i + PAIR] for i in range(0, scores.shape[1], PAIR)]
    top = functools.reduce(jnp.maximum, tiles)
    top = jnp.broadcast_to(jnp.max(top, axis=-1, keepdims=True), top.shape)
    if carried is not None:
        top = jnp.maximum(top, carried[1])
    raised = [jnp.exp(tile - top).astype(jnp.bfloat16) for tile in tiles]
    total = project(jnp.concatenate(raised, axis=1), own_lanes(head, value, 1.0))
    if carried is not None:
        total = total + carried[0] * jnp.exp(carried[1] - top)
    return total, top


def query_kernel(rows_ref, gain_ref, bias_ref, weight_ref, out_ref):
    rows = normed(rows_ref[...], gain_ref[...], bias_ref[...])
    query = project(rows, weight_ref[...]).astype(jnp.bfloat16)
    out_ref[...] = query * jnp.bfloat16(HEAD_DIM ** (-0.5))


def context_kernel(
    first_ref, rows_ref, own_ref, gain_ref, bias_ref, key_ref, value_ref, keys_ref, values_ref
):
    rows = jnp.where(first_ref[0] == 1, own_ref[...], rows_ref[...])
    rows = normed(rows, gain_ref[...], bias_ref[...])
    keys_ref[...] = project(rows, key_ref[...]).astype(jnp.bfloat16)
    values_ref[...] = project(rows, value_ref[...]).astype(jnp.bfloat16)


def heads_kernel(query_ref, keys_ref, values_ref, sum_ref, top_ref, *, heads):
    for place, head in enumerate(heads):
        pair = columns(head // 2)
        sum_ref[:, columns(place)], top_ref[:, columns(place)] = attend(
            head, query_ref[:, pair], keys_ref[:, pair], values_ref[:, pair]
        )


def state(refs, head):
    place = columns(head % HALF)
    sum_ref, top_ref = refs[:2] if head < HALF else refs[2:]
    return sum_ref.at[:, place], top_ref.at[:, place]


def own_context(rows_refs, gain_ref, bias_ref, key_ref, value_ref):
    rows = [ref[...] for ref in rows_refs]
    rows = rows[0] if len(rows) == 1 else jnp.concatenate(rows, axis=0)
    rows = normed(rows, gain_ref[...], bias_ref[...])
    keys = project(rows, key_ref[...]).astype(jnp.bfloat16)
    values = project(rows, value_ref[...]).astype(jnp.bfloat16)
    return keys, values


def more_kernel(query_ref, gain_ref, bias_ref, key_ref, value_ref, *refs):
    rows, carried, out = refs[:-8], refs[-8:-4], refs[-4:]
    keys, values = own_context(rows, gain_ref, bias_ref, key_ref, value_ref)
    for head in range(HEADS):
        pair = columns(head // 2)
        before = [ref[...] for ref in state(carried, head)]
        sum_ref, top_ref = state(out, head)
        sum_ref[...], top_ref[...] = attend(
            head, query_ref[:, pair], keys[:, pair], values[:, pair], before
        )


def last_kernel(query_ref, gain_ref, bias_ref, key_ref, value_ref, *refs):
    rows, carried = refs[:-9], refs[-9:-5]
    hidden_ref, out_weight_ref, out_bias_ref, out_ref, mixed_ref = refs[-5:]
    keys, values = own_context(rows, gain_ref, bias_ref, key_ref, value_ref)
    left = lanes_of(query_ref.shape[0]) < HEAD_DIM
    for pair in range(HEADS // 2):
        place = columns(pair)
        even, odd = (
            attend(
                head, query_ref[:, place], keys[:, place], values[:, place],
                [ref[...] for ref in state(carried, head)],
            )[0]
            for head in (2 * pair, 2 * pair + 1)
        )
        weight = pltpu.roll(jnp.where(left, odd, even), HEAD_DIM, 1)
        mixed_ref[:, place] = (jnp.where(left, even, odd) / weight).astype(jnp.bfloat16)
    for start in range(0, out_ref.shape[1], OUT_TILE):
        tile = slice(start, start + OUT_TILE)
        total = project(mixed_ref[...], out_weight_ref[:, tile])
        total = hidden_ref[:, tile].astype(jnp.float32) + total + out_bias_ref[:, tile]
        out_ref[:, tile] = total.astype(jnp.bfloat16)


def call(kernel, outs, *operands, scalars=0, flops=0, exps=0, aliases=None, scratch=()):
    whole = pl.BlockSpec(memory_space=pltpu.VMEM)
    specs = [pl.BlockSpec(memory_space=pltpu.SMEM)] * scalars
    return pl.pallas_call(
        kernel,
        out_shape=outs,
        in_specs=specs + [whole] * (len(operands) - scalars),
        out_specs=jax.tree.map(lambda _: whole, outs),
        scratch_shapes=scratch,
        input_output_aliases=aliases or {},
        compiler_params=pltpu.CompilerParams(vmem_limit_bytes=VMEM_BYTES),
        cost_estimate=pl.CostEstimate(flops=flops, bytes_accessed=1 << 20, transcendentals=exps),
    )(*operands)


def halves(tokens):
    return (jax.ShapeDtypeStruct((tokens, HALF * PAIR), jnp.float32),) * 2


def body(hidden_states, norm_gain, norm_bias, w_query, w_key, w_value, w_out, out_bias):
    position = lax.axis_index("grp") * lax.axis_size("frame") + lax.axis_index("frame")
    at_start = jnp.where(position == 0, 1, 0).astype(jnp.int32).reshape(1)
    norm = (norm_gain.reshape(1, -1), norm_bias.reshape(1, -1))
    tokens, width = hidden_states.shape
    inner = w_query.shape[1]
    narrow = jax.ShapeDtypeStruct((tokens, inner), jnp.bfloat16)
    tie = lax.optimization_barrier

    shifted = lax.ppermute(hidden_states, AXES, NEXT_FRAME)
    piece = scatter(hidden_states)
    query = call(
        query_kernel, narrow, hidden_states, *norm, w_query, flops=2 * tokens * width * inner
    )
    piece, query = tie((piece, query))
    piece = spread(piece, range(1, 4))

    piece, shifted = tie((piece, shifted))
    keys, values = call(
        context_kernel, (narrow, narrow), at_start, shifted, hidden_states, *norm, w_key, w_value,
        scalars=1, flops=4 * tokens * width * inner,
    )
    piece = spread(piece, [4])
    held = ()
    for half in range(2):
        piece, keys, values = tie((piece, keys, values))
        held += call(
            functools.partial(heads_kernel, heads=range(half * HALF, (half + 1) * HALF)),
            halves(tokens), query, keys, values,
            flops=8 * HALF * tokens * tokens * PAIR, exps=HALF * tokens * tokens,
        )
        piece = spread(piece, [5 + half])
        piece, held = tie((piece, held))

    def more(rows, held):
        return call(
            more_kernel, halves(tokens) * 2, query, *norm, w_key, w_value, *rows, *held,
            aliases={5 + len(rows) + i: i for i in range(4)}, flops=4 * tokens * width * inner,
        )

    come = lax.ppermute(piece, AXES, exchange(1))
    early = jnp.concatenate([piece, come], axis=0)
    early_other = lax.ppermute(early, AXES, CORE_SWAP)
    late = lax.ppermute(early, AXES, exchange(0))
    held = more([early, early_other], held)
    late, held = tie((late, held))
    late_other = lax.ppermute(late, AXES, CORE_SWAP)
    held = more([late], held)
    return call(
        last_kernel, jax.ShapeDtypeStruct((tokens, width), jnp.bfloat16),
        query, *norm, w_key, w_value, late_other, *held, hidden_states, w_out,
        out_bias.reshape(1, -1),
        flops=4 * tokens * width * inner, scratch=[pltpu.VMEM((tokens, inner), jnp.bfloat16)],
    )


def solution(mesh):
    placed = (P(AXES, None), P(), P(), P(), P(), P(), P(), P())
    return jax.shard_map(
        body, mesh=mesh, in_specs=placed, out_specs=P(AXES, None), check_vma=False
    )
```

```python
import functools

import jax
import jax.numpy as jnp
from jax import lax
from jax.experimental import pallas as pl
from jax.experimental.pallas import tpu as pltpu
from jax.sharding import PartitionSpec as P

HEADS = 10
HEAD_DIM = 64
PAIR = 2 * HEAD_DIM
GROUPS = ((0,), (1, 2), (3, 4))
OUT_TILE = 256
VMEM_BYTES = 16 << 20
AXES = ("grp", "frame")


SIZES = {"x": 4, "y": 4, "z": 8}

STEPS = {
    4: (((0, 1),), ((0, 3), (1, 2))),
    8: (((0, 3),), ((0, 6), (3, 4)), ((0, 1), (3, 2), (4, 5), (6, 7))),
}
ORDER = "zzzyy"


def device_index(place, core):
    if core == 1:
        place = {n: -v % SIZES[n] for n, v in place.items()}
    x, y, z = place["x"], place["y"], place["z"]
    return ((z // 4) * 4 + x) * 32 + ((z % 4) * 4 + y) * 2 + core


def tree():
    held = {"x": list(range(4)), "y": [0], "z": [0]}
    taken = {name: 0 for name in "xyz"}
    rounds = []
    for axis in ORDER:
        step = STEPS[SIZES[axis]][taken[axis]]
        taken[axis] += 1
        pairs = []
        for core in range(2):
            for x in held["x"]:
                for y in held["y"]:
                    for z in held["z"]:
                        place = {"x": x, "y": y, "z": z}
                        for source, sink in step:
                            if place[axis] == source:
                                pairs.append(
                                    (
                                        device_index(place, core),
                                        device_index({**place, axis: sink}, core),
                                    )
                                )
        before = {name: sum(1 << v for v in nodes) for name, nodes in held.items()}
        rounds.append((sorted(pairs), before))
        held[axis] = held[axis] + [sink for _, sink in step]
    assert all(len(held[name]) == SIZES[name] for name in "xyz")
    return rounds


def exchange(step):
    pairs = []
    for core in range(2):
        for y in range(4):
            for z in range(8):
                for a, b in (((0, 1), (2, 3)), ((0, 3), (1, 2)))[step]:
                    ends = [device_index({"x": v, "y": y, "z": z}, core) for v in (a, b)]
                    pairs += [(ends[0], ends[1]), (ends[1], ends[0])]
    return sorted(pairs)


CORE_SWAP = [(i, i ^ 1) for i in range(256)]
NEXT_FRAME = [(i, (i + 1) % 256) for i in range(256)]


def holding():
    grp, frame = lax.axis_index("grp"), lax.axis_index("frame")
    second = frame % 2 == 1
    place = {"x": grp % 4, "y": frame // 2 % 4, "z": grp // 4 * 4 + frame // 8}
    return second, {n: jnp.where(second, (SIZES[n] - v) % SIZES[n], v) for n, v in place.items()}


def flags(width):
    second, place = holding()
    answers = [
        jnp.where(second, 1, 0),
        jnp.where(lax.axis_index("grp") + lax.axis_index("frame") == 0, 1, 0),
        place["x"] % 2,
        place["x"] // 2,
    ]
    for _, before in tree():
        inside = [(before[n] >> place[n]) & 1 for n in "xyz"]
        answers.append(inside[0] * inside[1] * inside[2])
    bits = sum(answer << i for i, answer in enumerate(answers)).astype(jnp.int32)
    return jnp.full((8, width), bits)


def along_x(x):
    return [[device_index({"x": v, "y": 0, "z": 0}, core) for v in (0, x)] for core in range(2)]


def choose(bits_ref, index, yes, no):
    flag = (bits_ref[:1, :] >> index) & 1 == 1
    return jnp.where(flag, yes.astype(jnp.float32), no.astype(jnp.float32))


def split_kernel(bits_ref, rows_ref, other_ref, *refs):
    parts, token_ref = refs[:4], refs[4]
    size = parts[0].shape[0]
    for i, part in enumerate(parts):
        place = pl.ds(i * size, size)
        there = pl.ds((4 + i) * size, size)
        part[...] = choose(bits_ref, 0, other_ref[there, :], rows_ref[place, :]).astype(jnp.bfloat16)
    token_ref[...] = bits_ref[...]


def pick_kernel(bits_ref, zero_ref, one_ref, two_ref, three_ref, out_ref, token_ref):
    low = choose(bits_ref, 2, one_ref[...], zero_ref[...])
    high = choose(bits_ref, 2, three_ref[...], two_ref[...])
    out_ref[...] = choose(bits_ref, 3, high, low).astype(jnp.bfloat16)
    token_ref[...] = bits_ref[...]


def merge_kernel(bits_ref, piece_ref, come_ref, out_ref, token_ref, *, step):
    piece = choose(bits_ref, 4 + step, piece_ref[...], come_ref[...])
    out_ref[...] = piece.astype(jnp.bfloat16)
    token_ref[...] = bits_ref[...]


def pass_kernel(bits_ref, piece_ref, out_ref, token_ref):
    out_ref[...] = piece_ref[...]
    token_ref[...] = bits_ref[...]


def join_kernel(bits_ref, piece_ref, come_ref, out_ref, token_ref):
    out_ref[: piece_ref.shape[0], :] = piece_ref[...]
    out_ref[piece_ref.shape[0] :, :] = come_ref[...]
    token_ref[...] = bits_ref[...]


def normed(rows, gain, bias):
    values = rows.astype(jnp.float32)
    center = jnp.mean(values, axis=-1, keepdims=True)
    values = values - center
    spread = jnp.mean(values * values, axis=-1, keepdims=True)
    return (values * lax.rsqrt(spread + 1e-05) * gain + bias).astype(jnp.bfloat16)


def project(rows, weight):
    return jnp.dot(rows, weight, preferred_element_type=jnp.float32)


def lanes_of(rows):
    return lax.broadcasted_iota(jnp.int32, (rows, PAIR), 1)


def columns(index):
    return slice(index * PAIR, (index + 1) * PAIR)


def own_lanes(head, array, fill):
    left = lanes_of(array.shape[0]) < HEAD_DIM
    other = jnp.full(array.shape, fill, jnp.bfloat16)
    return jnp.where(left, array, other) if head % 2 == 0 else jnp.where(left, other, array)


def attend(head, query, key, value, carried=None):
    scores = lax.dot_general(
        query, own_lanes(head, key, 0.0), (((1,), (1,)), ((), ())),
        preferred_element_type=jnp.float32,
    )
    tiles = [scores[:, i : i + PAIR] for i in range(0, scores.shape[1], PAIR)]
    top = functools.reduce(jnp.maximum, tiles)
    top = jnp.broadcast_to(jnp.max(top, axis=-1, keepdims=True), top.shape)
    if carried is not None:
        top = jnp.maximum(top, carried[1])
    raised = [jnp.exp(tile - top).astype(jnp.bfloat16) for tile in tiles]
    total = project(jnp.concatenate(raised, axis=1), own_lanes(head, value, 1.0))
    if carried is not None:
        total = total + carried[0] * jnp.exp(carried[1] - top)
    return total, top


def query_kernel(bits_ref, rows_ref, gain_ref, bias_ref, weight_ref, out_ref, token_ref):
    rows = normed(rows_ref[...], gain_ref[...], bias_ref[...])
    query = project(rows, weight_ref[...]).astype(jnp.bfloat16)
    out_ref[...] = query * jnp.bfloat16(HEAD_DIM ** (-0.5))
    token_ref[...] = bits_ref[...]


def prior_kernel(*refs, pairs):
    if pairs == GROUPS[0]:
        bits_ref, rows_ref, own_ref, gain_ref, bias_ref = refs[:5]
        rows = choose(bits_ref, 1, own_ref[...], rows_ref[...])
        rows = normed(rows, gain_ref[...], bias_ref[...])
        refs[-2][...] = rows
        query_ref, key_ref, value_ref, sum_ref, top_ref = refs[5:10]
    else:
        bits_ref, rows_ref, query_ref, key_ref, value_ref, sum_ref, top_ref = refs[:7]
        rows = rows_ref[...]
    lanes = slice(pairs[0] * PAIR, (pairs[-1] + 1) * PAIR)
    keys = project(rows, key_ref[:, lanes]).astype(jnp.bfloat16)
    values = project(rows, value_ref[:, lanes]).astype(jnp.bfloat16)
    for place, head in enumerate(range(2 * pairs[0], 2 * pairs[-1] + 2)):
        pair = columns(place // 2)
        sum_ref[:, columns(place)], top_ref[:, columns(place)] = attend(
            head, query_ref[:, columns(head // 2)], keys[:, pair], values[:, pair]
        )
    refs[-1][...] = bits_ref[...]


def state(refs, head):
    for group, pairs in enumerate(GROUPS):
        if head // 2 in pairs:
            place = columns(head - 2 * pairs[0])
            return refs[2 * group].at[:, place], refs[2 * group + 1].at[:, place]


def own_context(rows_refs, gain_ref, bias_ref, key_ref, value_ref):
    rows = [ref[...] for ref in rows_refs]
    rows = rows[0] if len(rows) == 1 else jnp.concatenate(rows, axis=0)
    rows = normed(rows, gain_ref[...], bias_ref[...])
    keys = project(rows, key_ref[...]).astype(jnp.bfloat16)
    values = project(rows, value_ref[...]).astype(jnp.bfloat16)
    return keys, values


def more_kernel(bits_ref, query_ref, gain_ref, bias_ref, key_ref, value_ref, *refs):
    *refs, token_ref = refs
    size = 2 * len(GROUPS)
    rows, carried, out = refs[: -2 * size], refs[-2 * size : -size], refs[-size:]
    token_ref[...] = bits_ref[...]
    keys, values = own_context(rows, gain_ref, bias_ref, key_ref, value_ref)
    for head in range(HEADS):
        pair = columns(head // 2)
        before = [ref[...] for ref in state(carried, head)]
        sum_ref, top_ref = state(out, head)
        sum_ref[...], top_ref[...] = attend(
            head, query_ref[:, pair], keys[:, pair], values[:, pair], before
        )


def last_kernel(query_ref, gain_ref, bias_ref, key_ref, value_ref, *refs):
    rows, carried = refs[: -5 - 2 * len(GROUPS)], refs[-5 - 2 * len(GROUPS) : -5]
    hidden_ref, out_weight_ref, out_bias_ref, out_ref, mixed_ref = refs[-5:]
    keys, values = own_context(rows, gain_ref, bias_ref, key_ref, value_ref)
    left = lanes_of(query_ref.shape[0]) < HEAD_DIM
    for pair in range(HEADS // 2):
        place = columns(pair)
        even, odd = (
            attend(
                head, query_ref[:, place], keys[:, place], values[:, place],
                [ref[...] for ref in state(carried, head)],
            )[0]
            for head in (2 * pair, 2 * pair + 1)
        )
        weight = pltpu.roll(jnp.where(left, odd, even), HEAD_DIM, 1)
        mixed_ref[:, place] = (jnp.where(left, even, odd) / weight).astype(jnp.bfloat16)
    for start in range(0, out_ref.shape[1], OUT_TILE):
        tile = slice(start, start + OUT_TILE)
        total = project(mixed_ref[...], out_weight_ref[:, tile])
        total = hidden_ref[:, tile].astype(jnp.float32) + total + out_bias_ref[:, tile]
        out_ref[:, tile] = total.astype(jnp.bfloat16)


def call(kernel, outs, *operands, flops=0, exps=0, aliases=None, scratch=(), token=True):
    whole = pl.BlockSpec(memory_space=pltpu.VMEM)
    outs = tuple(outs)
    if token:
        outs += (jax.ShapeDtypeStruct(operands[0].shape, operands[0].dtype),)
    return pl.pallas_call(
        kernel,
        out_shape=outs,
        in_specs=[whole] * len(operands),
        out_specs=(whole,) * len(outs),
        scratch_shapes=scratch,
        input_output_aliases=aliases or {},
        compiler_params=pltpu.CompilerParams(vmem_limit_bytes=VMEM_BYTES),
        cost_estimate=pl.CostEstimate(flops=flops, bytes_accessed=1 << 18, transcendentals=exps),
    )(*operands)


def body(hidden_states, norm_gain, norm_bias, w_query, w_key, w_value, w_out, out_bias):
    norm = (norm_gain.reshape(1, -1), norm_bias.reshape(1, -1))
    tokens, width = hidden_states.shape
    inner = w_query.shape[1]
    quarter = tokens // 8
    bits = flags(width)
    rounds = tree()

    def rows_of(count):
        return jax.ShapeDtypeStruct((count, width), jnp.bfloat16)

    shifted = lax.ppermute(hidden_states, AXES, NEXT_FRAME)
    other = lax.ppermute(hidden_states, AXES, CORE_SWAP)
    *parts, bits = call(split_kernel, [rows_of(quarter)] * 4, bits, hidden_states, other)
    for x in (1, 3, 2):
        parts[x] = lax.ppermute(parts[x], AXES, along_x(x))
    query, bits = call(
        query_kernel, [jax.ShapeDtypeStruct((tokens, inner), jnp.bfloat16)],
        bits, hidden_states, *norm, w_query, flops=2 * tokens * width * inner,
    )
    piece, bits = call(pick_kernel, [rows_of(quarter)], bits, *parts)

    held = []
    for step, (pairs, _) in enumerate(rounds):
        come = lax.ppermute(piece, AXES, pairs)
        group = step - len(rounds) + len(GROUPS)
        if group >= 0:
            size = 2 * len(GROUPS[group])
            outs = [jax.ShapeDtypeStruct((tokens, size * PAIR), jnp.float32)] * 2
            rows = [shifted, hidden_states, *norm]
            if group > 0:
                rows = [prior]
            sum_, top, *made, bits = call(
                functools.partial(prior_kernel, pairs=GROUPS[group]),
                outs + [rows_of(tokens)] * (group == 0),
                bits, *rows, query, w_key, w_value,
                flops=4 * size * tokens * tokens * PAIR, exps=size * tokens * tokens,
            )
            held += [sum_, top]
            prior = made[0] if made else prior
        piece, bits = call(
            functools.partial(merge_kernel, step=step), [rows_of(quarter)], bits, piece, come
        )

    def more(bits, rows, held):
        *held, bits = call(
            more_kernel, [jax.ShapeDtypeStruct(h.shape, h.dtype) for h in held],
            bits, query, *norm, w_key, w_value, *rows, *held,
            aliases={6 + len(rows) + i: i for i in range(len(held))}, flops=4 * tokens * width * inner,
        )
        return held, bits

    come = lax.ppermute(piece, AXES, exchange(1))
    early, bits = call(join_kernel, [rows_of(2 * quarter)], bits, piece, come)
    early_other = lax.ppermute(early, AXES, CORE_SWAP)
    late = lax.ppermute(early, AXES, exchange(0))
    held, bits = more(bits, [early, early_other], held)
    late, bits = call(pass_kernel, [rows_of(2 * quarter)], bits, late)
    late_other = lax.ppermute(late, AXES, CORE_SWAP)
    held, bits = more(bits, [late], held)
    (out,) = call(
        last_kernel, [rows_of(tokens)],
        query, *norm, w_key, w_value, late_other, *held, hidden_states, w_out,
        out_bias.reshape(1, -1),
        flops=4 * tokens * width * inner, scratch=[pltpu.VMEM((tokens, inner), jnp.bfloat16)],
        token=False,
    )
    return out


def solution(mesh):
    placed = (P(AXES, None), P(), P(), P(), P(), P(), P(), P())
    return jax.shard_map(
        body, mesh=mesh, in_specs=placed, out_specs=P(AXES, None), check_vma=False
    )
```

```python
import functools

import jax
import jax.numpy as jnp
from jax import lax
from jax.experimental import pallas as pl
from jax.experimental.pallas import tpu as pltpu
from jax.sharding import PartitionSpec as P

HEADS = 10
HEAD_DIM = 64
PAIR = 2 * HEAD_DIM
GROUPS = ((0,), (1, 2), (3, 4))
OUT_TILE = 256
VMEM_BYTES = 16 << 20
AXES = ("grp", "frame")


SIZES = {"x": 4, "y": 4, "z": 8}

FIRST, SECOND = ((0, 1),), ((0, 3), (1, 2))
ROUNDS = (
    ({"x": FIRST}, {"y": FIRST}, {"x": FIRST, "y": FIRST}),
    ({"x": SECOND}, {"z": ((0, 3),)}, {"x": SECOND, "z": ((0, 3),)}),
    ({"y": SECOND}, {"z": ((0, 6), (3, 4))}, {"y": SECOND, "z": ((0, 6), (3, 4))}),
    ({"z": ((0, 1), (3, 2), (4, 5), (6, 7))},),
)


def device_index(place, core):
    if core == 1:
        place = {n: -v % SIZES[n] for n, v in place.items()}
    x, y, z = place["x"], place["y"], place["z"]
    return ((z // 4) * 4 + x) * 32 + ((z % 4) * 4 + y) * 2 + core


def chips():
    return [{"x": x, "y": y, "z": z} for x in range(4) for y in range(4) for z in range(8)]


def plan():
    held = {name: [0] for name in "xyz"}
    rounds = []
    for sends in ROUNDS:
        made = []
        for send in sends:
            pairs = []
            for chip in chips():
                moves = {n: dict(send[n]) for n in send}
                if all(chip[n] in held[n] for n in "xyz") and all(chip[n] in moves[n] for n in send):
                    sink = {**chip, **{n: moves[n][chip[n]] for n in send}}
                    pairs += [(device_index(chip, c), device_index(sink, c)) for c in range(2)]
            sinks = {n: [to for _, to in send[n]] if n in send else held[n] for n in "xyz"}
            made.append((sorted(pairs), {n: sum(1 << v for v in sinks[n]) for n in "xyz"}))
        for send in sends:
            held = {
                n: sorted(set(held[n]) | {to for _, to in send.get(n, ())}) for n in "xyz"
            }
        rounds.append(made)
    assert all(len(held[n]) == SIZES[n] for n in "xyz")
    return rounds


def exchange(axis):
    pairs = []
    for chip in chips():
        other = {**chip, axis: chip[axis] ^ 1}
        pairs += [(device_index(chip, core), device_index(other, core)) for core in range(2)]
    return sorted(pairs)


CORE_SWAP = [(i, i ^ 1) for i in range(256)]
NEXT_FRAME = [(i, (i + 1) % 256) for i in range(256)]


def flags(rounds, width):
    grp, frame = lax.axis_index("grp"), lax.axis_index("frame")
    second = frame % 2
    place = {"x": grp % 4, "y": frame // 2 % 4, "z": grp // 4 * 4 + frame // 8}
    place = {n: jnp.where(second == 1, (SIZES[n] - v) % SIZES[n], v) for n, v in place.items()}
    bits = second + jnp.where(grp + frame == 0, 2, 0)
    for step, sends in enumerate(rounds):
        for which, (_, sinks) in enumerate(sends):
            inside = [(sinks[n] >> place[n]) & 1 for n in "xyz"]
            bits += (inside[0] * inside[1] * inside[2] * (which + 1)) << (2 + 2 * step)
    return jnp.full((8, width), bits.astype(jnp.int32))


def choose(bits_ref, index, yes, no):
    flag = (bits_ref[:1, :] >> index) & 1 == 1
    return jnp.where(flag, yes.astype(jnp.float32), no.astype(jnp.float32))


def low_kernel(bits_ref, rows_ref, low_ref, token_ref):
    low_ref[...] = rows_ref[: low_ref.shape[0], :]
    token_ref[...] = bits_ref[...]


def split_kernel(bits_ref, rows_ref, other_ref, *refs):
    *parts, token_ref = refs
    size = parts[0].shape[0]
    for i, part in enumerate(parts):
        place, there = pl.ds(i * size, size), pl.ds((4 + i) * size, size)
        part[...] = choose(bits_ref, 0, other_ref[there, :], rows_ref[place, :]).astype(jnp.bfloat16)
    token_ref[...] = bits_ref[...]


def pick_kernel(bits_ref, *refs, step, count):
    parts, outs, token_ref = refs[:count], refs[count:-1], refs[-1]
    piece = choose(bits_ref, 2 + 2 * step, parts[1][...], parts[0][...])
    if count == 4:
        high = choose(bits_ref, 2 + 2 * step, parts[3][...], parts[2][...])
        piece = choose(bits_ref, 3 + 2 * step, high, piece)
    piece = piece.astype(jnp.bfloat16)
    size = outs[0].shape[0]
    for i, out in enumerate(outs):
        out[...] = piece[i * size : (i + 1) * size, :]
    token_ref[...] = bits_ref[...]


def join_kernel(bits_ref, *refs, count, each):
    parts, outs, token_ref = refs[:count], refs[count:-1], refs[-1]
    start = 0
    for i, part in enumerate(parts):
        rows = part.shape[0]
        outs[0][start : start + rows, :] = part[...]
        start += rows
        if each:
            outs[1 + i // 2][i % 2 * rows : (i % 2 + 1) * rows, :] = part[...]
    token_ref[...] = bits_ref[...]


def normed(rows, gain, bias):
    values = rows.astype(jnp.float32)
    center = jnp.mean(values, axis=-1, keepdims=True)
    values = values - center
    spread = jnp.mean(values * values, axis=-1, keepdims=True)
    return (values * lax.rsqrt(spread + 1e-05) * gain + bias).astype(jnp.bfloat16)


def project(rows, weight):
    return jnp.dot(rows, weight, preferred_element_type=jnp.float32)


def lanes_of(rows):
    return lax.broadcasted_iota(jnp.int32, (rows, PAIR), 1)


def columns(index):
    return slice(index * PAIR, (index + 1) * PAIR)


def own_lanes(head, array, fill):
    left = lanes_of(array.shape[0]) < HEAD_DIM
    other = jnp.full(array.shape, fill, jnp.bfloat16)
    return jnp.where(left, array, other) if head % 2 == 0 else jnp.where(left, other, array)


def attend(head, query, key, value, carried=None):
    scores = lax.dot_general(
        query, own_lanes(head, key, 0.0), (((1,), (1,)), ((), ())),
        preferred_element_type=jnp.float32,
    )
    tiles = [scores[:, i : i + PAIR] for i in range(0, scores.shape[1], PAIR)]
    top = functools.reduce(jnp.maximum, tiles)
    top = jnp.broadcast_to(jnp.max(top, axis=-1, keepdims=True), top.shape)
    if carried is not None:
        top = jnp.maximum(top, carried[1])
    raised = [jnp.exp(tile - top).astype(jnp.bfloat16) for tile in tiles]
    total = project(jnp.concatenate(raised, axis=1), own_lanes(head, value, 1.0))
    if carried is not None:
        total = total + carried[0] * jnp.exp(carried[1] - top)
    return total, top


def query_kernel(bits_ref, rows_ref, gain_ref, bias_ref, weight_ref, out_ref, token_ref):
    rows = normed(rows_ref[...], gain_ref[...], bias_ref[...])
    query = project(rows, weight_ref[...]).astype(jnp.bfloat16)
    out_ref[...] = query * jnp.bfloat16(HEAD_DIM ** (-0.5))
    token_ref[...] = bits_ref[...]


def prior_kernel(*refs, pairs):
    if pairs == GROUPS[0]:
        bits_ref, rows_ref, own_ref, gain_ref, bias_ref = refs[:5]
        rows = choose(bits_ref, 1, own_ref[...], rows_ref[...])
        rows = normed(rows, gain_ref[...], bias_ref[...])
        refs[-2][...] = rows
        query_ref, key_ref, value_ref, sum_ref, top_ref = refs[5:10]
    else:
        bits_ref, rows_ref, query_ref, key_ref, value_ref, sum_ref, top_ref = refs[:7]
        rows = rows_ref[...]
    lanes = slice(pairs[0] * PAIR, (pairs[-1] + 1) * PAIR)
    keys = project(rows, key_ref[:, lanes]).astype(jnp.bfloat16)
    values = project(rows, value_ref[:, lanes]).astype(jnp.bfloat16)
    for place, head in enumerate(range(2 * pairs[0], 2 * pairs[-1] + 2)):
        pair = columns(place // 2)
        sum_ref[:, columns(place)], top_ref[:, columns(place)] = attend(
            head, query_ref[:, columns(head // 2)], keys[:, pair], values[:, pair]
        )
    refs[-1][...] = bits_ref[...]


def state(refs, head):
    for group, pairs in enumerate(GROUPS):
        if head // 2 in pairs:
            place = columns(head - 2 * pairs[0])
            return refs[2 * group].at[:, place], refs[2 * group + 1].at[:, place]


def context(rows_refs, gain_ref, bias_ref, key_ref, value_ref):
    rows = [ref[...] for ref in rows_refs]
    rows = rows[0] if len(rows) == 1 else jnp.concatenate(rows, axis=0)
    rows = normed(rows, gain_ref[...], bias_ref[...])
    keys = project(rows, key_ref[...]).astype(jnp.bfloat16)
    values = project(rows, value_ref[...]).astype(jnp.bfloat16)
    return keys, values


def context_kernel(
    bits_ref, rows_ref, gain_ref, bias_ref, key_ref, value_ref, keys_ref, values_ref, token_ref
):
    keys_ref[...], values_ref[...] = context([rows_ref], gain_ref, bias_ref, key_ref, value_ref)
    token_ref[...] = bits_ref[...]


def more_kernel(bits_ref, query_ref, gain_ref, bias_ref, key_ref, value_ref, *refs):
    *refs, token_ref = refs
    size = 2 * len(GROUPS)
    rows, carried, out = refs[: -2 * size], refs[-2 * size : -size], refs[-size:]
    keys, values = context(rows, gain_ref, bias_ref, key_ref, value_ref)
    for head in range(HEADS):
        pair = columns(head // 2)
        before = [ref[...] for ref in state(carried, head)]
        sum_ref, top_ref = state(out, head)
        sum_ref[...], top_ref[...] = attend(
            head, query_ref[:, pair], keys[:, pair], values[:, pair], before
        )
    token_ref[...] = bits_ref[...]


def last_kernel(
    bits_ref, query_ref, gain_ref, bias_ref, key_ref, value_ref, rows_ref, keys_ref, values_ref,
    hidden_ref, out_weight_ref, out_bias_ref, *refs,
):
    *carried, out_ref, mixed_ref = refs
    keys, values = context([rows_ref], gain_ref, bias_ref, key_ref, value_ref)
    keys = jnp.concatenate([keys_ref[...], keys], axis=0)
    values = jnp.concatenate([values_ref[...], values], axis=0)
    left = lanes_of(query_ref.shape[0]) < HEAD_DIM
    for pair in range(HEADS // 2):
        place = columns(pair)
        even, odd = (
            attend(
                head, query_ref[:, place], keys[:, place], values[:, place],
                [ref[...] for ref in state(carried, head)],
            )[0]
            for head in (2 * pair, 2 * pair + 1)
        )
        weight = pltpu.roll(jnp.where(left, odd, even), HEAD_DIM, 1)
        mixed_ref[:, place] = (jnp.where(left, even, odd) / weight).astype(jnp.bfloat16)
    for start in range(0, out_ref.shape[1], OUT_TILE):
        tile = slice(start, start + OUT_TILE)
        total = project(mixed_ref[...], out_weight_ref[:, tile])
        total = hidden_ref[:, tile].astype(jnp.float32) + total + out_bias_ref[:, tile]
        out_ref[:, tile] = total.astype(jnp.bfloat16)


def call(kernel, outs, *operands, flops=0, exps=0, aliases=None, scratch=(), token=True):
    whole = pl.BlockSpec(memory_space=pltpu.VMEM)
    outs = tuple(outs)
    if token:
        outs += (jax.ShapeDtypeStruct(operands[0].shape, operands[0].dtype),)
    return pl.pallas_call(
        kernel,
        out_shape=outs,
        in_specs=[whole] * len(operands),
        out_specs=(whole,) * len(outs),
        scratch_shapes=scratch,
        input_output_aliases=aliases or {},
        compiler_params=pltpu.CompilerParams(vmem_limit_bytes=VMEM_BYTES),
        cost_estimate=pl.CostEstimate(flops=flops, bytes_accessed=1 << 18, transcendentals=exps),
    )(*operands)


def body(hidden_states, norm_gain, norm_bias, w_query, w_key, w_value, w_out, out_bias):
    norm = (norm_gain.reshape(1, -1), norm_bias.reshape(1, -1))
    tokens, width = hidden_states.shape
    inner = w_query.shape[1]
    rounds = plan()
    bits = flags(rounds, width)

    def array(rows, columns=width, dtype=jnp.bfloat16):
        return jax.ShapeDtypeStruct((rows, columns), dtype)

    def move(value, pairs):
        return lax.ppermute(value, AXES, pairs)

    def prior(bits, group, rows):
        size = 2 * len(GROUPS[group])
        return call(
            functools.partial(prior_kernel, pairs=GROUPS[group]),
            [array(tokens, size * PAIR, jnp.float32)] * 2 + [array(tokens)] * (group == 0),
            bits, *rows, query, w_key, w_value,
            flops=4 * size * tokens * tokens * PAIR, exps=size * tokens * tokens,
        )

    shifted = move(hidden_states, NEXT_FRAME)
    other = move(hidden_states, CORE_SWAP)
    low, bits = call(low_kernel, [array(tokens // 2)], bits, hidden_states)
    *parts, bits = call(split_kernel, [array(tokens // 8)] * 4, bits, low, other)
    for step, sends in enumerate(rounds):
        come = [move(parts[which + 1 if step == 0 else 0], sent[0]) for which, sent in enumerate(sends)]
        if step == 0:
            query, bits = call(
                query_kernel, [array(tokens, inner)], bits, hidden_states, *norm, w_query,
                flops=2 * tokens * width * inner,
            )
        if step == 2:
            *held, rows, bits = prior(bits, 0, [shifted, hidden_states, *norm])
        if step == 3:
            *sums, bits = prior(bits, 1, [rows])
            held += sums
        outs = 2 if step == len(rounds) - 1 else 1
        *parts, bits = call(
            functools.partial(pick_kernel, step=step, count=1 + len(sends)),
            [array(tokens // 8 // outs)] * outs, bits, parts[0], *come,
        )

    first, second = parts
    first_come, second_come = move(first, exchange("x")), move(second, exchange("y"))
    *sums, bits = prior(bits, 2, [rows])
    held += sums
    early, first, second, bits = call(
        functools.partial(join_kernel, count=4, each=True),
        [array(tokens // 4), array(tokens // 8), array(tokens // 8)],
        bits, first, first_come, second, second_come,
    )
    first_come, second_come = move(first, exchange("y")), move(second, exchange("x"))
    early_other = move(early, CORE_SWAP)
    *held, bits = call(
        more_kernel, [jax.ShapeDtypeStruct(h.shape, h.dtype) for h in held],
        bits, query, *norm, w_key, w_value, early, early_other, *held,
        aliases={8 + i: i for i in range(len(held))}, flops=4 * tokens * width * inner,
    )
    late, bits = call(
        functools.partial(join_kernel, count=2, each=False), [array(tokens // 4)],
        bits, first_come, second_come,
    )
    late_other = move(late, CORE_SWAP)
    keys, values, bits = call(
        context_kernel, [array(tokens // 4, inner)] * 2, bits, late, *norm, w_key, w_value,
        flops=tokens * width * inner,
    )
    (out,) = call(
        last_kernel, [array(tokens)],
        bits, query, *norm, w_key, w_value, late_other, keys, values,
        hidden_states, w_out, out_bias.reshape(1, -1), *held,
        flops=4 * tokens * width * inner, scratch=[pltpu.VMEM((tokens, inner), jnp.bfloat16)],
        token=False,
    )
    return out


def solution(mesh):
    placed = (P(AXES, None), P(), P(), P(), P(), P(), P(), P())
    return jax.shard_map(
        body, mesh=mesh, in_specs=placed, out_specs=P(AXES, None), check_vma=False
    )
```

```python
import functools

import jax
import jax.numpy as jnp
from jax import lax
from jax.experimental import pallas as pl
from jax.experimental.pallas import tpu as pltpu
from jax.sharding import PartitionSpec as P

HEADS = 10
HEAD_DIM = 64
PAIR = 2 * HEAD_DIM
GROUPS = ((0,), (1, 2), (3, 4))
OUT_TILE = 256
VMEM_BYTES = 16 << 20
AXES = ("grp", "frame")


SIZES = {"x": 4, "y": 4, "z": 8}

FIRST, SECOND = ((0, 1),), ((0, 3), (1, 2))
ROUNDS = (
    ({"x": FIRST}, {"y": FIRST}, {"x": FIRST, "y": FIRST}),
    ({"x": SECOND}, {"z": ((0, 1),)}, {"x": SECOND, "z": ((0, 1),)}),
    ({"y": SECOND}, {"z": ((0, 6), (1, 3))}, {"y": SECOND, "z": ((0, 6), (1, 3))}),
    ({"z": ((0, 7), (1, 2), (3, 4), (6, 5))},),
)


def device_index(place, core):
    if core == 1:
        place = {n: -v % SIZES[n] for n, v in place.items()}
    x, y, z = place["x"], place["y"], place["z"]
    return ((z // 4) * 4 + x) * 32 + ((z % 4) * 4 + y) * 2 + core


def chips():
    return [{"x": x, "y": y, "z": z} for x in range(4) for y in range(4) for z in range(8)]


def plan():
    held = {name: [0] for name in "xyz"}
    rounds = []
    for sends in ROUNDS:
        made = []
        for send in sends:
            pairs = []
            for chip in chips():
                moves = {n: dict(send[n]) for n in send}
                if all(chip[n] in held[n] for n in "xyz") and all(chip[n] in moves[n] for n in send):
                    sink = {**chip, **{n: moves[n][chip[n]] for n in send}}
                    pairs += [(device_index(chip, c), device_index(sink, c)) for c in range(2)]
            sinks = {n: [to for _, to in send[n]] if n in send else held[n] for n in "xyz"}
            made.append((sorted(pairs), {n: sum(1 << v for v in sinks[n]) for n in "xyz"}))
        for send in sends:
            held = {
                n: sorted(set(held[n]) | {to for _, to in send.get(n, ())}) for n in "xyz"
            }
        rounds.append(made)
    assert all(len(held[n]) == SIZES[n] for n in "xyz")
    return rounds


def exchange(axis):
    pairs = []
    for chip in chips():
        other = {**chip, axis: chip[axis] ^ 1}
        pairs += [(device_index(chip, core), device_index(other, core)) for core in range(2)]
    return sorted(pairs)


CORE_SWAP = [(i, i ^ 1) for i in range(256)]
NEXT_FRAME = [(i, (i + 1) % 256) for i in range(256)]


def flags(rounds, width):
    grp, frame = lax.axis_index("grp"), lax.axis_index("frame")
    second = frame % 2
    place = {"x": grp % 4, "y": frame // 2 % 4, "z": grp // 4 * 4 + frame // 8}
    place = {n: jnp.where(second == 1, (SIZES[n] - v) % SIZES[n], v) for n, v in place.items()}
    bits = second + jnp.where(grp + frame == 0, 2, 0)
    for step, sends in enumerate(rounds):
        for which, (_, sinks) in enumerate(sends):
            inside = [(sinks[n] >> place[n]) & 1 for n in "xyz"]
            bits += (inside[0] * inside[1] * inside[2] * (which + 1)) << (2 + 2 * step)
    return jnp.full((8, width), bits.astype(jnp.int32))


def choose(bits_ref, index, yes, no):
    flag = (bits_ref[:1, :] >> index) & 1 == 1
    return jnp.where(flag, yes.astype(jnp.float32), no.astype(jnp.float32))


def low_kernel(bits_ref, rows_ref, low_ref, token_ref):
    low_ref[...] = rows_ref[: low_ref.shape[0], :]
    token_ref[...] = bits_ref[...]


def split_kernel(bits_ref, rows_ref, other_ref, *refs):
    *parts, token_ref = refs
    size = parts[0].shape[0]
    for i, part in enumerate(parts):
        place, there = pl.ds(i * size, size), pl.ds((4 + i) * size, size)
        part[...] = choose(bits_ref, 0, other_ref[there, :], rows_ref[place, :]).astype(jnp.bfloat16)
    token_ref[...] = bits_ref[...]


def pick_kernel(bits_ref, *refs, step, count):
    parts, outs, token_ref = refs[:count], refs[count:-1], refs[-1]
    piece = choose(bits_ref, 2 + 2 * step, parts[1][...], parts[0][...])
    if count == 4:
        high = choose(bits_ref, 2 + 2 * step, parts[3][...], parts[2][...])
        piece = choose(bits_ref, 3 + 2 * step, high, piece)
    piece = piece.astype(jnp.bfloat16)
    size = outs[0].shape[0]
    for i, out in enumerate(outs):
        out[...] = piece[i * size : (i + 1) * size, :]
    token_ref[...] = bits_ref[...]


def join_kernel(bits_ref, *refs, count, each):
    parts, outs, token_ref = refs[:count], refs[count:-1], refs[-1]
    start = 0
    for i, part in enumerate(parts):
        rows = part.shape[0]
        outs[0][start : start + rows, :] = part[...]
        start += rows
        if each:
            outs[1 + i // 2][i % 2 * rows : (i % 2 + 1) * rows, :] = part[...]
    token_ref[...] = bits_ref[...]


def normed(rows, gain, bias):
    values = rows.astype(jnp.float32)
    center = jnp.mean(values, axis=-1, keepdims=True)
    values = values - center
    spread = jnp.mean(values * values, axis=-1, keepdims=True)
    return (values * lax.rsqrt(spread + 1e-05) * gain + bias).astype(jnp.bfloat16)


def project(rows, weight):
    return jnp.dot(rows, weight, preferred_element_type=jnp.float32)


def lanes_of(rows):
    return lax.broadcasted_iota(jnp.int32, (rows, PAIR), 1)


def columns(index):
    return slice(index * PAIR, (index + 1) * PAIR)


def own_lanes(head, array, fill):
    left = lanes_of(array.shape[0]) < HEAD_DIM
    other = jnp.full(array.shape, fill, jnp.bfloat16)
    return jnp.where(left, array, other) if head % 2 == 0 else jnp.where(left, other, array)


def attend(head, query, key, value, carried=None):
    scores = lax.dot_general(
        query, own_lanes(head, key, 0.0), (((1,), (1,)), ((), ())),
        preferred_element_type=jnp.float32,
    )
    tiles = [scores[:, i : i + PAIR] for i in range(0, scores.shape[1], PAIR)]
    top = functools.reduce(jnp.maximum, tiles)
    top = jnp.broadcast_to(jnp.max(top, axis=-1, keepdims=True), top.shape)
    if carried is not None:
        top = jnp.maximum(top, carried[1])
    raised = [jnp.exp(tile - top).astype(jnp.bfloat16) for tile in tiles]
    total = project(jnp.concatenate(raised, axis=1), own_lanes(head, value, 1.0))
    if carried is not None:
        total = total + carried[0] * jnp.exp(carried[1] - top)
    return total, top


def query_kernel(bits_ref, rows_ref, gain_ref, bias_ref, weight_ref, out_ref, token_ref):
    rows = normed(rows_ref[...], gain_ref[...], bias_ref[...])
    query = project(rows, weight_ref[...]).astype(jnp.bfloat16)
    out_ref[...] = query * jnp.bfloat16(HEAD_DIM ** (-0.5))
    token_ref[...] = bits_ref[...]


def prior_kernel(*refs, pairs):
    if pairs == GROUPS[0]:
        bits_ref, rows_ref, own_ref, gain_ref, bias_ref = refs[:5]
        rows = choose(bits_ref, 1, own_ref[...], rows_ref[...])
        rows = normed(rows, gain_ref[...], bias_ref[...])
        refs[-2][...] = rows
        query_ref, key_ref, value_ref, sum_ref, top_ref = refs[5:10]
    else:
        bits_ref, rows_ref, query_ref, key_ref, value_ref, sum_ref, top_ref = refs[:7]
        rows = rows_ref[...]
    lanes = slice(pairs[0] * PAIR, (pairs[-1] + 1) * PAIR)
    keys = project(rows, key_ref[:, lanes]).astype(jnp.bfloat16)
    values = project(rows, value_ref[:, lanes]).astype(jnp.bfloat16)
    for place, head in enumerate(range(2 * pairs[0], 2 * pairs[-1] + 2)):
        pair = columns(place // 2)
        sum_ref[:, columns(place)], top_ref[:, columns(place)] = attend(
            head, query_ref[:, columns(head // 2)], keys[:, pair], values[:, pair]
        )
    refs[-1][...] = bits_ref[...]


def state(refs, head):
    for group, pairs in enumerate(GROUPS):
        if head // 2 in pairs:
            place = columns(head - 2 * pairs[0])
            return refs[2 * group].at[:, place], refs[2 * group + 1].at[:, place]


def context(rows_refs, gain_ref, bias_ref, key_ref, value_ref):
    rows = [ref[...] for ref in rows_refs]
    rows = rows[0] if len(rows) == 1 else jnp.concatenate(rows, axis=0)
    rows = normed(rows, gain_ref[...], bias_ref[...])
    keys = project(rows, key_ref[...]).astype(jnp.bfloat16)
    values = project(rows, value_ref[...]).astype(jnp.bfloat16)
    return keys, values


def context_kernel(
    bits_ref, rows_ref, gain_ref, bias_ref, key_ref, value_ref, keys_ref, values_ref, token_ref
):
    keys_ref[...], values_ref[...] = context([rows_ref], gain_ref, bias_ref, key_ref, value_ref)
    token_ref[...] = bits_ref[...]


def more_kernel(bits_ref, query_ref, gain_ref, bias_ref, key_ref, value_ref, *refs):
    *refs, token_ref = refs
    size = 2 * len(GROUPS)
    rows, carried, out = refs[: -2 * size], refs[-2 * size : -size], refs[-size:]
    keys, values = context(rows, gain_ref, bias_ref, key_ref, value_ref)
    for head in range(HEADS):
        pair = columns(head // 2)
        before = [ref[...] for ref in state(carried, head)]
        sum_ref, top_ref = state(out, head)
        sum_ref[...], top_ref[...] = attend(
            head, query_ref[:, pair], keys[:, pair], values[:, pair], before
        )
    token_ref[...] = bits_ref[...]


def last_kernel(
    bits_ref, query_ref, gain_ref, bias_ref, key_ref, value_ref, rows_ref, keys_ref, values_ref,
    hidden_ref, out_weight_ref, out_bias_ref, *refs,
):
    *carried, out_ref, mixed_ref = refs
    keys, values = context([rows_ref], gain_ref, bias_ref, key_ref, value_ref)
    keys = jnp.concatenate([keys_ref[...], keys], axis=0)
    values = jnp.concatenate([values_ref[...], values], axis=0)
    left = lanes_of(query_ref.shape[0]) < HEAD_DIM
    for pair in range(HEADS // 2):
        place = columns(pair)
        even, odd = (
            attend(
                head, query_ref[:, place], keys[:, place], values[:, place],
                [ref[...] for ref in state(carried, head)],
            )[0]
            for head in (2 * pair, 2 * pair + 1)
        )
        weight = pltpu.roll(jnp.where(left, odd, even), HEAD_DIM, 1)
        mixed_ref[:, place] = (jnp.where(left, even, odd) / weight).astype(jnp.bfloat16)
    for start in range(0, out_ref.shape[1], OUT_TILE):
        tile = slice(start, start + OUT_TILE)
        total = project(mixed_ref[...], out_weight_ref[:, tile])
        total = hidden_ref[:, tile].astype(jnp.float32) + total + out_bias_ref[:, tile]
        out_ref[:, tile] = total.astype(jnp.bfloat16)


def call(kernel, outs, *operands, flops=0, exps=0, aliases=None, scratch=(), token=True):
    whole = pl.BlockSpec(memory_space=pltpu.VMEM)
    outs = tuple(outs)
    if token:
        outs += (jax.ShapeDtypeStruct(operands[0].shape, operands[0].dtype),)
    return pl.pallas_call(
        kernel,
        out_shape=outs,
        in_specs=[whole] * len(operands),
        out_specs=(whole,) * len(outs),
        scratch_shapes=scratch,
        input_output_aliases=aliases or {},
        compiler_params=pltpu.CompilerParams(vmem_limit_bytes=VMEM_BYTES),
        cost_estimate=pl.CostEstimate(flops=flops, bytes_accessed=1 << 18, transcendentals=exps),
    )(*operands)


def body(hidden_states, norm_gain, norm_bias, w_query, w_key, w_value, w_out, out_bias):
    norm = (norm_gain.reshape(1, -1), norm_bias.reshape(1, -1))
    tokens, width = hidden_states.shape
    inner = w_query.shape[1]
    rounds = plan()
    bits = flags(rounds, width)

    def array(rows, columns=width, dtype=jnp.bfloat16):
        return jax.ShapeDtypeStruct((rows, columns), dtype)

    def move(value, pairs):
        return lax.ppermute(value, AXES, pairs)

    def prior(bits, group, rows):
        size = 2 * len(GROUPS[group])
        return call(
            functools.partial(prior_kernel, pairs=GROUPS[group]),
            [array(tokens, size * PAIR, jnp.float32)] * 2 + [array(tokens)] * (group == 0),
            bits, *rows, query, w_key, w_value,
            flops=4 * size * tokens * tokens * PAIR, exps=size * tokens * tokens,
        )

    shifted = move(hidden_states, NEXT_FRAME)
    other = move(hidden_states, CORE_SWAP)
    low, bits = call(low_kernel, [array(tokens // 2)], bits, hidden_states)
    *parts, bits = call(split_kernel, [array(tokens // 8)] * 4, bits, low, other)
    for step, sends in enumerate(rounds):
        come = [move(parts[which + 1 if step == 0 else 0], sent[0]) for which, sent in enumerate(sends)]
        if step == 0:
            query, bits = call(
                query_kernel, [array(tokens, inner)], bits, hidden_states, *norm, w_query,
                flops=2 * tokens * width * inner,
            )
        if step == 2:
            *held, rows, bits = prior(bits, 0, [shifted, hidden_states, *norm])
        if step == 3:
            *sums, bits = prior(bits, 1, [rows])
            held += sums
        outs = 2 if step == len(rounds) - 1 else 1
        *parts, bits = call(
            functools.partial(pick_kernel, step=step, count=1 + len(sends)),
            [array(tokens // 8 // outs)] * outs, bits, parts[0], *come,
        )

    first, second = parts
    first_come, second_come = move(first, exchange("x")), move(second, exchange("y"))
    *sums, bits = prior(bits, 2, [rows])
    held += sums
    early, first, second, bits = call(
        functools.partial(join_kernel, count=4, each=True),
        [array(tokens // 4), array(tokens // 8), array(tokens // 8)],
        bits, first, first_come, second, second_come,
    )
    first_come, second_come = move(first, exchange("y")), move(second, exchange("x"))
    early_other = move(early, CORE_SWAP)
    *held, bits = call(
        more_kernel, [jax.ShapeDtypeStruct(h.shape, h.dtype) for h in held],
        bits, query, *norm, w_key, w_value, early, early_other, *held,
        aliases={8 + i: i for i in range(len(held))}, flops=4 * tokens * width * inner,
    )
    late, bits = call(
        functools.partial(join_kernel, count=2, each=False), [array(tokens // 4)],
        bits, first_come, second_come,
    )
    late_other = move(late, CORE_SWAP)
    keys, values, bits = call(
        context_kernel, [array(tokens // 4, inner)] * 2, bits, late, *norm, w_key, w_value,
        flops=tokens * width * inner,
    )
    (out,) = call(
        last_kernel, [array(tokens)],
        bits, query, *norm, w_key, w_value, late_other, keys, values,
        hidden_states, w_out, out_bias.reshape(1, -1), *held,
        flops=4 * tokens * width * inner, scratch=[pltpu.VMEM((tokens, inner), jnp.bfloat16)],
        token=False,
    )
    return out


def solution(mesh):
    placed = (P(AXES, None), P(), P(), P(), P(), P(), P(), P())
    return jax.shard_map(
        body, mesh=mesh, in_specs=placed, out_specs=P(AXES, None), check_vma=False
    )
```

```python
import functools

import jax
import jax.numpy as jnp
from jax import lax
from jax.experimental import pallas as pl
from jax.experimental.pallas import tpu as pltpu
from jax.sharding import PartitionSpec as P

HEADS = 10
HEAD_DIM = 64
PAIR = 2 * HEAD_DIM
GROUPS = ((0, 1), (2, 3), (4,))
OUT_TILE = 256
VMEM_BYTES = 16 << 20
AXES = ("grp", "frame")


SIZES = {"x": 4, "y": 4, "z": 8}

FIRST, SECOND = ((0, 1),), ((0, 3), (1, 2))
ROUNDS = (
    ({"x": FIRST}, {"y": FIRST}, {"x": FIRST, "y": FIRST}),
    ({"x": SECOND}, {"z": ((0, 1),)}, {"x": SECOND, "z": ((0, 1),)}),
    ({"y": SECOND}, {"z": ((0, 6), (1, 3))}, {"y": SECOND, "z": ((0, 6), (1, 3))}),
    ({"z": ((0, 7), (1, 2), (3, 4), (6, 5))},),
)


def device_index(place, core):
    if core == 1:
        place = {n: -v % SIZES[n] for n, v in place.items()}
    x, y, z = place["x"], place["y"], place["z"]
    return ((z // 4) * 4 + x) * 32 + ((z % 4) * 4 + y) * 2 + core


def chips():
    return [{"x": x, "y": y, "z": z} for x in range(4) for y in range(4) for z in range(8)]


def plan():
    held = {name: [0] for name in "xyz"}
    rounds = []
    for sends in ROUNDS:
        made = []
        for send in sends:
            pairs = []
            for chip in chips():
                moves = {n: dict(send[n]) for n in send}
                if all(chip[n] in held[n] for n in "xyz") and all(chip[n] in moves[n] for n in send):
                    sink = {**chip, **{n: moves[n][chip[n]] for n in send}}
                    pairs += [(device_index(chip, c), device_index(sink, c)) for c in range(2)]
            sinks = {n: [to for _, to in send[n]] if n in send else held[n] for n in "xyz"}
            made.append((sorted(pairs), {n: sum(1 << v for v in sinks[n]) for n in "xyz"}))
        for send in sends:
            held = {
                n: sorted(set(held[n]) | {to for _, to in send.get(n, ())}) for n in "xyz"
            }
        rounds.append(made)
    assert all(len(held[n]) == SIZES[n] for n in "xyz")
    return rounds


def exchange(axis):
    pairs = []
    for chip in chips():
        other = {**chip, axis: chip[axis] ^ 1}
        pairs += [(device_index(chip, core), device_index(other, core)) for core in range(2)]
    return sorted(pairs)


CORE_SWAP = [(i, i ^ 1) for i in range(256)]
NEXT_FRAME = [(i, (i + 1) % 256) for i in range(256)]


def flags(rounds, width):
    grp, frame = lax.axis_index("grp"), lax.axis_index("frame")
    second = frame % 2
    place = {"x": grp % 4, "y": frame // 2 % 4, "z": grp // 4 * 4 + frame // 8}
    place = {n: jnp.where(second == 1, (SIZES[n] - v) % SIZES[n], v) for n, v in place.items()}
    bits = second + jnp.where(grp + frame == 0, 2, 0)
    for step, sends in enumerate(rounds):
        for which, (_, sinks) in enumerate(sends):
            inside = [(sinks[n] >> place[n]) & 1 for n in "xyz"]
            bits += (inside[0] * inside[1] * inside[2] * (which + 1)) << (2 + 2 * step)
    return jnp.full((8, width), bits.astype(jnp.int32))


def choose(bits_ref, index, yes, no):
    flag = (bits_ref[:1, :] >> index) & 1 == 1
    return jnp.where(flag, yes.astype(jnp.float32), no.astype(jnp.float32))


def low_kernel(bits_ref, rows_ref, low_ref, token_ref):
    low_ref[...] = rows_ref[: low_ref.shape[0], :]
    token_ref[...] = bits_ref[...]


def split_kernel(bits_ref, rows_ref, other_ref, *refs):
    *parts, token_ref = refs
    size = parts[0].shape[0]
    for i, part in enumerate(parts):
        place, there = pl.ds(i * size, size), pl.ds((4 + i) * size, size)
        part[...] = choose(bits_ref, 0, other_ref[there, :], rows_ref[place, :]).astype(jnp.bfloat16)
    token_ref[...] = bits_ref[...]


def pick_kernel(bits_ref, *refs, step, count):
    parts, outs, token_ref = refs[:count], refs[count:-1], refs[-1]
    piece = choose(bits_ref, 2 + 2 * step, parts[1][...], parts[0][...])
    if count == 4:
        high = choose(bits_ref, 2 + 2 * step, parts[3][...], parts[2][...])
        piece = choose(bits_ref, 3 + 2 * step, high, piece)
    piece = piece.astype(jnp.bfloat16)
    size = outs[0].shape[0]
    for i, out in enumerate(outs):
        out[...] = piece[i * size : (i + 1) * size, :]
    token_ref[...] = bits_ref[...]


def join_kernel(bits_ref, *refs, count, each):
    parts, outs, token_ref = refs[:count], refs[count:-1], refs[-1]
    start = 0
    for i, part in enumerate(parts):
        rows = part.shape[0]
        outs[0][start : start + rows, :] = part[...]
        start += rows
        if each:
            outs[1 + i // 2][i % 2 * rows : (i % 2 + 1) * rows, :] = part[...]
    token_ref[...] = bits_ref[...]


def normed(rows, gain, bias):
    values = rows.astype(jnp.float32)
    center = jnp.mean(values, axis=-1, keepdims=True)
    values = values - center
    spread = jnp.mean(values * values, axis=-1, keepdims=True)
    return (values * lax.rsqrt(spread + 1e-05) * gain + bias).astype(jnp.bfloat16)


def project(rows, weight):
    return jnp.dot(rows, weight, preferred_element_type=jnp.float32)


def lanes_of(rows):
    return lax.broadcasted_iota(jnp.int32, (rows, PAIR), 1)


def columns(index):
    return slice(index * PAIR, (index + 1) * PAIR)


def own_lanes(head, array, fill):
    left = lanes_of(array.shape[0]) < HEAD_DIM
    other = jnp.full(array.shape, fill, jnp.bfloat16)
    return jnp.where(left, array, other) if head % 2 == 0 else jnp.where(left, other, array)


def attend(head, query, key, value, carried=None):
    scores = lax.dot_general(
        query, own_lanes(head, key, 0.0), (((1,), (1,)), ((), ())),
        preferred_element_type=jnp.float32,
    )
    tiles = [scores[:, i : i + PAIR] for i in range(0, scores.shape[1], PAIR)]
    top = functools.reduce(jnp.maximum, tiles)
    top = jnp.broadcast_to(jnp.max(top, axis=-1, keepdims=True), top.shape)
    if carried is not None:
        top = jnp.maximum(top, carried[1])
    raised = [jnp.exp(tile - top).astype(jnp.bfloat16) for tile in tiles]
    total = project(jnp.concatenate(raised, axis=1), own_lanes(head, value, 1.0))
    if carried is not None:
        total = total + carried[0] * jnp.exp(carried[1] - top)
    return total, top


def query_kernel(bits_ref, rows_ref, gain_ref, bias_ref, weight_ref, out_ref, token_ref):
    rows = normed(rows_ref[...], gain_ref[...], bias_ref[...])
    query = project(rows, weight_ref[...]).astype(jnp.bfloat16)
    out_ref[...] = query * jnp.bfloat16(HEAD_DIM ** (-0.5))
    token_ref[...] = bits_ref[...]


def prior_kernel(*refs, pairs):
    if pairs == GROUPS[0]:
        bits_ref, rows_ref, own_ref, gain_ref, bias_ref = refs[:5]
        rows = choose(bits_ref, 1, own_ref[...], rows_ref[...])
        rows = normed(rows, gain_ref[...], bias_ref[...])
        refs[-2][...] = rows
        query_ref, key_ref, value_ref, sum_ref, top_ref = refs[5:10]
    else:
        bits_ref, rows_ref, query_ref, key_ref, value_ref, sum_ref, top_ref = refs[:7]
        rows = rows_ref[...]
    lanes = slice(pairs[0] * PAIR, (pairs[-1] + 1) * PAIR)
    keys = project(rows, key_ref[:, lanes]).astype(jnp.bfloat16)
    values = project(rows, value_ref[:, lanes]).astype(jnp.bfloat16)
    for place, head in enumerate(range(2 * pairs[0], 2 * pairs[-1] + 2)):
        pair = columns(place // 2)
        sum_ref[:, columns(place)], top_ref[:, columns(place)] = attend(
            head, query_ref[:, columns(head // 2)], keys[:, pair], values[:, pair]
        )
    refs[-1][...] = bits_ref[...]


def state(refs, head):
    for group, pairs in enumerate(GROUPS):
        if head // 2 in pairs:
            place = columns(head - 2 * pairs[0])
            return refs[2 * group].at[:, place], refs[2 * group + 1].at[:, place]


def context(rows_refs, gain_ref, bias_ref, key_ref, value_ref):
    rows = [ref[...] for ref in rows_refs]
    rows = rows[0] if len(rows) == 1 else jnp.concatenate(rows, axis=0)
    rows = normed(rows, gain_ref[...], bias_ref[...])
    keys = project(rows, key_ref[...]).astype(jnp.bfloat16)
    values = project(rows, value_ref[...]).astype(jnp.bfloat16)
    return keys, values


def context_kernel(
    bits_ref, rows_ref, gain_ref, bias_ref, key_ref, value_ref, keys_ref, values_ref, token_ref
):
    keys_ref[...], values_ref[...] = context([rows_ref], gain_ref, bias_ref, key_ref, value_ref)
    token_ref[...] = bits_ref[...]


def more_kernel(bits_ref, query_ref, gain_ref, bias_ref, key_ref, value_ref, *refs):
    *refs, token_ref = refs
    size = 2 * len(GROUPS)
    rows, carried, out = refs[: -2 * size], refs[-2 * size : -size], refs[-size:]
    keys, values = context(rows, gain_ref, bias_ref, key_ref, value_ref)
    for head in range(HEADS):
        pair = columns(head // 2)
        before = [ref[...] for ref in state(carried, head)]
        sum_ref, top_ref = state(out, head)
        sum_ref[...], top_ref[...] = attend(
            head, query_ref[:, pair], keys[:, pair], values[:, pair], before
        )
    token_ref[...] = bits_ref[...]


def last_kernel(
    bits_ref, query_ref, gain_ref, bias_ref, key_ref, value_ref, rows_ref, keys_ref, values_ref,
    hidden_ref, out_weight_ref, out_bias_ref, *refs,
):
    *carried, out_ref, mixed_ref = refs
    keys, values = context([rows_ref], gain_ref, bias_ref, key_ref, value_ref)
    keys = jnp.concatenate([keys_ref[...], keys], axis=0)
    values = jnp.concatenate([values_ref[...], values], axis=0)
    left = lanes_of(query_ref.shape[0]) < HEAD_DIM
    for pair in range(HEADS // 2):
        place = columns(pair)
        even, odd = (
            attend(
                head, query_ref[:, place], keys[:, place], values[:, place],
                [ref[...] for ref in state(carried, head)],
            )[0]
            for head in (2 * pair, 2 * pair + 1)
        )
        weight = pltpu.roll(jnp.where(left, odd, even), HEAD_DIM, 1)
        mixed_ref[:, place] = (jnp.where(left, even, odd) / weight).astype(jnp.bfloat16)
    for start in range(0, out_ref.shape[1], OUT_TILE):
        tile = slice(start, start + OUT_TILE)
        total = project(mixed_ref[...], out_weight_ref[:, tile])
        total = hidden_ref[:, tile].astype(jnp.float32) + total + out_bias_ref[:, tile]
        out_ref[:, tile] = total.astype(jnp.bfloat16)


def call(kernel, outs, *operands, flops=0, exps=0, aliases=None, scratch=(), token=True):
    whole = pl.BlockSpec(memory_space=pltpu.VMEM)
    outs = tuple(outs)
    if token:
        outs += (jax.ShapeDtypeStruct(operands[0].shape, operands[0].dtype),)
    return pl.pallas_call(
        kernel,
        out_shape=outs,
        in_specs=[whole] * len(operands),
        out_specs=(whole,) * len(outs),
        scratch_shapes=scratch,
        input_output_aliases=aliases or {},
        compiler_params=pltpu.CompilerParams(vmem_limit_bytes=VMEM_BYTES),
        cost_estimate=pl.CostEstimate(flops=flops, bytes_accessed=1 << 18, transcendentals=exps),
    )(*operands)


def body(hidden_states, norm_gain, norm_bias, w_query, w_key, w_value, w_out, out_bias):
    norm = (norm_gain.reshape(1, -1), norm_bias.reshape(1, -1))
    tokens, width = hidden_states.shape
    inner = w_query.shape[1]
    rounds = plan()
    bits = flags(rounds, width)

    def array(rows, columns=width, dtype=jnp.bfloat16):
        return jax.ShapeDtypeStruct((rows, columns), dtype)

    def move(value, pairs):
        return lax.ppermute(value, AXES, pairs)

    def prior(bits, group, rows):
        size = 2 * len(GROUPS[group])
        return call(
            functools.partial(prior_kernel, pairs=GROUPS[group]),
            [array(tokens, size * PAIR, jnp.float32)] * 2 + [array(tokens)] * (group == 0),
            bits, *rows, query, w_key, w_value,
            flops=4 * size * tokens * tokens * PAIR, exps=size * tokens * tokens,
        )

    shifted = move(hidden_states, NEXT_FRAME)
    other = move(hidden_states, CORE_SWAP)
    low, bits = call(low_kernel, [array(tokens // 2)], bits, hidden_states)
    *parts, bits = call(split_kernel, [array(tokens // 8)] * 4, bits, low, other)
    for step, sends in enumerate(rounds):
        come = [move(parts[which + 1 if step == 0 else 0], sent[0]) for which, sent in enumerate(sends)]
        if step == 0:
            query, bits = call(
                query_kernel, [array(tokens, inner)], bits, hidden_states, *norm, w_query,
                flops=2 * tokens * width * inner,
            )
        if step == 2:
            *held, rows, bits = prior(bits, 0, [shifted, hidden_states, *norm])
        if step == 3:
            *sums, bits = prior(bits, 1, [rows])
            held += sums
        outs = 2 if step == len(rounds) - 1 else 1
        *parts, bits = call(
            functools.partial(pick_kernel, step=step, count=1 + len(sends)),
            [array(tokens // 8 // outs)] * outs, bits, parts[0], *come,
        )

    first, second = parts
    first_come, second_come = move(first, exchange("x")), move(second, exchange("y"))
    *sums, bits = prior(bits, 2, [rows])
    held += sums
    early, first, second, bits = call(
        functools.partial(join_kernel, count=4, each=True),
        [array(tokens // 4), array(tokens // 8), array(tokens // 8)],
        bits, first, first_come, second, second_come,
    )
    first_come, second_come = move(first, exchange("y")), move(second, exchange("x"))
    early_other = move(early, CORE_SWAP)
    *held, bits = call(
        more_kernel, [jax.ShapeDtypeStruct(h.shape, h.dtype) for h in held],
        bits, query, *norm, w_key, w_value, early, early_other, *held,
        aliases={8 + i: i for i in range(len(held))}, flops=4 * tokens * width * inner,
    )
    late, bits = call(
        functools.partial(join_kernel, count=2, each=False), [array(tokens // 4)],
        bits, first_come, second_come,
    )
    late_other = move(late, CORE_SWAP)
    keys, values, bits = call(
        context_kernel, [array(tokens // 4, inner)] * 2, bits, late, *norm, w_key, w_value,
        flops=tokens * width * inner,
    )
    (out,) = call(
        last_kernel, [array(tokens)],
        bits, query, *norm, w_key, w_value, late_other, keys, values,
        hidden_states, w_out, out_bias.reshape(1, -1), *held,
        flops=4 * tokens * width * inner, scratch=[pltpu.VMEM((tokens, inner), jnp.bfloat16)],
        token=False,
    )
    return out


def solution(mesh):
    placed = (P(AXES, None), P(), P(), P(), P(), P(), P(), P())
    return jax.shard_map(
        body, mesh=mesh, in_specs=placed, out_specs=P(AXES, None), check_vma=False
    )
```

```python
import functools

import jax
import jax.numpy as jnp
from jax import lax
from jax.experimental import pallas as pl
from jax.experimental.pallas import tpu as pltpu
from jax.sharding import PartitionSpec as P

HEADS = 10
HEAD_DIM = 64
PAIR = 2 * HEAD_DIM
GROUPS = ((0,), (1, 2), (3, 4))
OUT_TILE = 256
VMEM_BYTES = 16 << 20
AXES = ("grp", "frame")


SIZES = {"x": 4, "y": 4, "z": 8}

FIRST, SECOND = ((0, 1),), ((0, 3), (1, 2))
ROUNDS = (
    ({"x": FIRST}, {"y": FIRST}, {"x": FIRST, "y": FIRST}),
    ({"x": SECOND, "z": ((0, 1),)}, {"x": SECOND}, {"z": ((0, 1),)}),
    ({"y": SECOND}, {"z": ((0, 6), (1, 3))}, {"y": SECOND, "z": ((0, 6), (1, 3))}),
    ({"z": ((0, 7), (1, 2), (3, 4), (6, 5))},),
)


def device_index(place, core):
    if core == 1:
        place = {n: -v % SIZES[n] for n, v in place.items()}
    x, y, z = place["x"], place["y"], place["z"]
    return ((z // 4) * 4 + x) * 32 + ((z % 4) * 4 + y) * 2 + core


def chips():
    return [{"x": x, "y": y, "z": z} for x in range(4) for y in range(4) for z in range(8)]


def plan():
    held = {name: [0] for name in "xyz"}
    rounds = []
    for sends in ROUNDS:
        made = []
        for send in sends:
            pairs = []
            for chip in chips():
                moves = {n: dict(send[n]) for n in send}
                if all(chip[n] in held[n] for n in "xyz") and all(chip[n] in moves[n] for n in send):
                    sink = {**chip, **{n: moves[n][chip[n]] for n in send}}
                    pairs += [(device_index(chip, c), device_index(sink, c)) for c in range(2)]
            sinks = {n: [to for _, to in send[n]] if n in send else held[n] for n in "xyz"}
            made.append((sorted(pairs), {n: sum(1 << v for v in sinks[n]) for n in "xyz"}))
        for send in sends:
            held = {
                n: sorted(set(held[n]) | {to for _, to in send.get(n, ())}) for n in "xyz"
            }
        rounds.append(made)
    assert all(len(held[n]) == SIZES[n] for n in "xyz")
    return rounds


def exchange(axis):
    pairs = []
    for chip in chips():
        other = {**chip, axis: chip[axis] ^ 1}
        pairs += [(device_index(chip, core), device_index(other, core)) for core in range(2)]
    return sorted(pairs)


CORE_SWAP = [(i, i ^ 1) for i in range(256)]
NEXT_FRAME = [(i, (i + 1) % 256) for i in range(256)]


def flags(rounds, width):
    grp, frame = lax.axis_index("grp"), lax.axis_index("frame")
    second = frame % 2
    place = {"x": grp % 4, "y": frame // 2 % 4, "z": grp // 4 * 4 + frame // 8}
    place = {n: jnp.where(second == 1, (SIZES[n] - v) % SIZES[n], v) for n, v in place.items()}
    bits = second + jnp.where(grp + frame == 0, 2, 0)
    for step, sends in enumerate(rounds):
        for which, (_, sinks) in enumerate(sends):
            inside = [(sinks[n] >> place[n]) & 1 for n in "xyz"]
            bits += (inside[0] * inside[1] * inside[2] * (which + 1)) << (2 + 2 * step)
    return jnp.full((8, width), bits.astype(jnp.int32))


def choose(bits_ref, index, yes, no):
    flag = (bits_ref[:1, :] >> index) & 1 == 1
    return jnp.where(flag, yes.astype(jnp.float32), no.astype(jnp.float32))


def low_kernel(bits_ref, rows_ref, low_ref, token_ref):
    low_ref[...] = rows_ref[: low_ref.shape[0], :]
    token_ref[...] = bits_ref[...]


def split_kernel(bits_ref, rows_ref, other_ref, *refs):
    *parts, token_ref = refs
    size = parts[0].shape[0]
    for i, part in enumerate(parts):
        place, there = pl.ds(i * size, size), pl.ds((4 + i) * size, size)
        part[...] = choose(bits_ref, 0, other_ref[there, :], rows_ref[place, :]).astype(jnp.bfloat16)
    token_ref[...] = bits_ref[...]


def pick_kernel(bits_ref, *refs, step, count):
    parts, outs, token_ref = refs[:count], refs[count:-1], refs[-1]
    piece = choose(bits_ref, 2 + 2 * step, parts[1][...], parts[0][...])
    if count == 4:
        high = choose(bits_ref, 2 + 2 * step, parts[3][...], parts[2][...])
        piece = choose(bits_ref, 3 + 2 * step, high, piece)
    piece = piece.astype(jnp.bfloat16)
    size = outs[0].shape[0]
    for i, out in enumerate(outs):
        out[...] = piece[i * size : (i + 1) * size, :]
    token_ref[...] = bits_ref[...]


def join_kernel(bits_ref, *refs, count, each):
    parts, outs, token_ref = refs[:count], refs[count:-1], refs[-1]
    start = 0
    for i, part in enumerate(parts):
        rows = part.shape[0]
        outs[0][start : start + rows, :] = part[...]
        start += rows
        if each:
            outs[1 + i // 2][i % 2 * rows : (i % 2 + 1) * rows, :] = part[...]
    token_ref[...] = bits_ref[...]


def normed(rows, gain, bias):
    values = rows.astype(jnp.float32)
    center = jnp.mean(values, axis=-1, keepdims=True)
    values = values - center
    spread = jnp.mean(values * values, axis=-1, keepdims=True)
    return (values * lax.rsqrt(spread + 1e-05) * gain + bias).astype(jnp.bfloat16)


def project(rows, weight):
    return jnp.dot(rows, weight, preferred_element_type=jnp.float32)


def lanes_of(rows):
    return lax.broadcasted_iota(jnp.int32, (rows, PAIR), 1)


def columns(index):
    return slice(index * PAIR, (index + 1) * PAIR)


def own_lanes(head, array, fill):
    left = lanes_of(array.shape[0]) < HEAD_DIM
    other = jnp.full(array.shape, fill, jnp.bfloat16)
    return jnp.where(left, array, other) if head % 2 == 0 else jnp.where(left, other, array)


def attend(head, query, key, value, carried=None):
    scores = lax.dot_general(
        query, own_lanes(head, key, 0.0), (((1,), (1,)), ((), ())),
        preferred_element_type=jnp.float32,
    )
    tiles = [scores[:, i : i + PAIR] for i in range(0, scores.shape[1], PAIR)]
    top = functools.reduce(jnp.maximum, tiles)
    top = jnp.broadcast_to(jnp.max(top, axis=-1, keepdims=True), top.shape)
    if carried is not None:
        top = jnp.maximum(top, carried[1])
    raised = [jnp.exp(tile - top).astype(jnp.bfloat16) for tile in tiles]
    total = project(jnp.concatenate(raised, axis=1), own_lanes(head, value, 1.0))
    if carried is not None:
        total = total + carried[0] * jnp.exp(carried[1] - top)
    return total, top


def query_kernel(bits_ref, rows_ref, gain_ref, bias_ref, weight_ref, out_ref, token_ref):
    rows = normed(rows_ref[...], gain_ref[...], bias_ref[...])
    query = project(rows, weight_ref[...]).astype(jnp.bfloat16)
    out_ref[...] = query * jnp.bfloat16(HEAD_DIM ** (-0.5))
    token_ref[...] = bits_ref[...]


def prior_kernel(*refs, pairs):
    if pairs == GROUPS[0]:
        bits_ref, rows_ref, own_ref, gain_ref, bias_ref = refs[:5]
        rows = choose(bits_ref, 1, own_ref[...], rows_ref[...])
        rows = normed(rows, gain_ref[...], bias_ref[...])
        refs[-2][...] = rows
        query_ref, key_ref, value_ref, sum_ref, top_ref = refs[5:10]
    else:
        bits_ref, rows_ref, query_ref, key_ref, value_ref, sum_ref, top_ref = refs[:7]
        rows = rows_ref[...]
    lanes = slice(pairs[0] * PAIR, (pairs[-1] + 1) * PAIR)
    keys = project(rows, key_ref[:, lanes]).astype(jnp.bfloat16)
    values = project(rows, value_ref[:, lanes]).astype(jnp.bfloat16)
    for place, head in enumerate(range(2 * pairs[0], 2 * pairs[-1] + 2)):
        pair = columns(place // 2)
        sum_ref[:, columns(place)], top_ref[:, columns(place)] = attend(
            head, query_ref[:, columns(head // 2)], keys[:, pair], values[:, pair]
        )
    refs[-1][...] = bits_ref[...]


def state(refs, head):
    for group, pairs in enumerate(GROUPS):
        if head // 2 in pairs:
            place = columns(head - 2 * pairs[0])
            return refs[2 * group].at[:, place], refs[2 * group + 1].at[:, place]


def context(rows_refs, gain_ref, bias_ref, key_ref, value_ref):
    rows = [ref[...] for ref in rows_refs]
    rows = rows[0] if len(rows) == 1 else jnp.concatenate(rows, axis=0)
    rows = normed(rows, gain_ref[...], bias_ref[...])
    keys = project(rows, key_ref[...]).astype(jnp.bfloat16)
    values = project(rows, value_ref[...]).astype(jnp.bfloat16)
    return keys, values


def context_kernel(
    bits_ref, rows_ref, gain_ref, bias_ref, key_ref, value_ref, keys_ref, values_ref, token_ref
):
    keys_ref[...], values_ref[...] = context([rows_ref], gain_ref, bias_ref, key_ref, value_ref)
    token_ref[...] = bits_ref[...]


def more_kernel(bits_ref, query_ref, gain_ref, bias_ref, key_ref, value_ref, *refs):
    *refs, token_ref = refs
    size = 2 * len(GROUPS)
    rows, carried, out = refs[: -2 * size], refs[-2 * size : -size], refs[-size:]
    keys, values = context(rows, gain_ref, bias_ref, key_ref, value_ref)
    for head in range(HEADS):
        pair = columns(head // 2)
        before = [ref[...] for ref in state(carried, head)]
        sum_ref, top_ref = state(out, head)
        sum_ref[...], top_ref[...] = attend(
            head, query_ref[:, pair], keys[:, pair], values[:, pair], before
        )
    token_ref[...] = bits_ref[...]


def last_kernel(
    bits_ref, query_ref, gain_ref, bias_ref, key_ref, value_ref, rows_ref, keys_ref, values_ref,
    hidden_ref, out_weight_ref, out_bias_ref, *refs,
):
    *carried, out_ref, mixed_ref = refs
    keys, values = context([rows_ref], gain_ref, bias_ref, key_ref, value_ref)
    keys = jnp.concatenate([keys_ref[...], keys], axis=0)
    values = jnp.concatenate([values_ref[...], values], axis=0)
    left = lanes_of(query_ref.shape[0]) < HEAD_DIM
    for pair in range(HEADS // 2):
        place = columns(pair)
        even, odd = (
            attend(
                head, query_ref[:, place], keys[:, place], values[:, place],
                [ref[...] for ref in state(carried, head)],
            )[0]
            for head in (2 * pair, 2 * pair + 1)
        )
        weight = pltpu.roll(jnp.where(left, odd, even), HEAD_DIM, 1)
        mixed_ref[:, place] = (jnp.where(left, even, odd) / weight).astype(jnp.bfloat16)
    for start in range(0, out_ref.shape[1], OUT_TILE):
        tile = slice(start, start + OUT_TILE)
        total = project(mixed_ref[...], out_weight_ref[:, tile])
        total = hidden_ref[:, tile].astype(jnp.float32) + total + out_bias_ref[:, tile]
        out_ref[:, tile] = total.astype(jnp.bfloat16)


def call(kernel, outs, *operands, flops=0, exps=0, aliases=None, scratch=(), token=True):
    whole = pl.BlockSpec(memory_space=pltpu.VMEM)
    outs = tuple(outs)
    if token:
        outs += (jax.ShapeDtypeStruct(operands[0].shape, operands[0].dtype),)
    return pl.pallas_call(
        kernel,
        out_shape=outs,
        in_specs=[whole] * len(operands),
        out_specs=(whole,) * len(outs),
        scratch_shapes=scratch,
        input_output_aliases=aliases or {},
        compiler_params=pltpu.CompilerParams(vmem_limit_bytes=VMEM_BYTES),
        cost_estimate=pl.CostEstimate(flops=flops, bytes_accessed=1 << 18, transcendentals=exps),
    )(*operands)


def body(hidden_states, norm_gain, norm_bias, w_query, w_key, w_value, w_out, out_bias):
    norm = (norm_gain.reshape(1, -1), norm_bias.reshape(1, -1))
    tokens, width = hidden_states.shape
    inner = w_query.shape[1]
    rounds = plan()
    bits = flags(rounds, width)

    def array(rows, columns=width, dtype=jnp.bfloat16):
        return jax.ShapeDtypeStruct((rows, columns), dtype)

    def move(value, pairs):
        return lax.ppermute(value, AXES, pairs)

    def prior(bits, group, rows):
        size = 2 * len(GROUPS[group])
        return call(
            functools.partial(prior_kernel, pairs=GROUPS[group]),
            [array(tokens, size * PAIR, jnp.float32)] * 2 + [array(tokens)] * (group == 0),
            bits, *rows, query, w_key, w_value,
            flops=4 * size * tokens * tokens * PAIR, exps=size * tokens * tokens,
        )

    shifted = move(hidden_states, NEXT_FRAME)
    other = move(hidden_states, CORE_SWAP)
    low, bits = call(low_kernel, [array(tokens // 2)], bits, hidden_states)
    *parts, bits = call(split_kernel, [array(tokens // 8)] * 4, bits, low, other)
    for step, sends in enumerate(rounds):
        come = [move(parts[which + 1 if step == 0 else 0], sent[0]) for which, sent in enumerate(sends)]
        if step == 0:
            query, bits = call(
                query_kernel, [array(tokens, inner)], bits, hidden_states, *norm, w_query,
                flops=2 * tokens * width * inner,
            )
        if step == 2:
            *held, rows, bits = prior(bits, 0, [shifted, hidden_states, *norm])
        if step == 3:
            *sums, bits = prior(bits, 1, [rows])
            held += sums
        outs = 2 if step == len(rounds) - 1 else 1
        *parts, bits = call(
            functools.partial(pick_kernel, step=step, count=1 + len(sends)),
            [array(tokens // 8 // outs)] * outs, bits, parts[0], *come,
        )

    first, second = parts
    first_come, second_come = move(first, exchange("x")), move(second, exchange("y"))
    *sums, bits = prior(bits, 2, [rows])
    held += sums
    early, first, second, bits = call(
        functools.partial(join_kernel, count=4, each=True),
        [array(tokens // 4), array(tokens // 8), array(tokens // 8)],
        bits, first, first_come, second, second_come,
    )
    first_come, second_come = move(first, exchange("y")), move(second, exchange("x"))
    early_other = move(early, CORE_SWAP)
    *held, bits = call(
        more_kernel, [jax.ShapeDtypeStruct(h.shape, h.dtype) for h in held],
        bits, query, *norm, w_key, w_value, early, early_other, *held,
        aliases={8 + i: i for i in range(len(held))}, flops=4 * tokens * width * inner,
    )
    late, bits = call(
        functools.partial(join_kernel, count=2, each=False), [array(tokens // 4)],
        bits, first_come, second_come,
    )
    late_other = move(late, CORE_SWAP)
    keys, values, bits = call(
        context_kernel, [array(tokens // 4, inner)] * 2, bits, late, *norm, w_key, w_value,
        flops=tokens * width * inner,
    )
    (out,) = call(
        last_kernel, [array(tokens)],
        bits, query, *norm, w_key, w_value, late_other, keys, values,
        hidden_states, w_out, out_bias.reshape(1, -1), *held,
        flops=4 * tokens * width * inner, scratch=[pltpu.VMEM((tokens, inner), jnp.bfloat16)],
        token=False,
    )
    return out


def solution(mesh):
    placed = (P(AXES, None), P(), P(), P(), P(), P(), P(), P())
    return jax.shard_map(
        body, mesh=mesh, in_specs=placed, out_specs=P(AXES, None), check_vma=False
    )
```
